32 devices in a mesh: group: 2 (over x), tm: 2 (over core), space: 8 (over z, y).
Axes of the slice: x: 2, y: 2, z: 4, core: 2. Of those that a mesh axis runs over, the one named last changes fastest.
Arguments:
- start_old: float32 [4, 3, 1024, 1024], P(('group', 'tm'), None, 'space'), parts along dimension 0, may hold values from -3 to 3
- incoming: float32 [6, 512, 512], P('group', 'space'), parts along dimension 0, may hold values from -3 to 3
Outputs:
- new_states: float32 [4, 3, 1024, 1024], P(('group', 'tm'), None, 'space'), parts along dimension 0
The draws below stay inside these ranges and needn't reach their ends.
There are 2 independent parts, one for each index of `group`. The reference program is written for one: setup_inputs(seed, part) draws one part's arguments, and reference() takes and returns one part's arrays. A program takes and returns all parts, laid end to end along the dimension named above; each array names one. Nothing has to cross between parts.
All inputs are finite; a program needn't handle non-finite values.
Results may differ from the reference program's by a relative error of at most 0.0001.
Values sent between devices are 32-bit elements; how exact they have to be, the bound alone decides.
A program may use at most 192 MiB of HBM per device.

```python
import math
import jax
import jax.numpy as jnp
from jax import lax

NC = 512
RATIO = 2
STEPS = 2
SLICES = 2
NF = 1024


def steps_of(stream_key, shape, pieces, low, high):
    gain = 1.0
    for dim, shards_of in pieces:
        steps = jax.random.uniform(jax.random.fold_in(jax.random.fold_in(stream_key, 6), dim), (shards_of,), jnp.float32, low / len(pieces), high / len(pieces))
        gain = gain * jnp.repeat(jnp.exp(steps), shape[dim] // shards_of).reshape((-1,) + (1,) * (len(shape) - 1 - dim))
    return gain


def centred(own_key, shape, scale, most, split=(), kind=jnp.bfloat16):
    result = jax.random.normal(own_key, shape, jnp.float32) * scale
    if len(split) > 0:
        result = steps_of(own_key, shape, split, -0.22, 0.18) * result
    return jnp.clip(result, min=-most, max=most).astype(kind)


def setup_inputs(seed: int = 0, part: int = 0) -> dict:
    streams_of = jax.random.split(jax.random.key(seed), 3)
    part_splits = jax.random.split(jax.random.fold_in(streams_of[2], part), 3)
    return {
        "start_old": centred(part_splits[0], (SLICES, 3, NF, NF), 0.5, 3.0, ((0, 2), (2, 8)), jnp.float32),
        "incoming": centred(part_splits[1], (3, NC, NC), 0.5, 3.0, ((1, 8),), jnp.float32),
    }


TIME_STEP = 0.25
CORIOLIS = 0.5
GRAVITY = 1.0
MEAN_DEPTH = 1.0

def slope_east(field):
    return 0.5 * (jnp.roll(field, -1, -1) - jnp.roll(field, 1, -1))

def slope_north(field):
    return 0.5 * (jnp.roll(field, -1, -2) - jnp.roll(field, 1, -2))

def tendency(state):
    column_depth = MEAN_DEPTH + state[0]
    flux_east = column_depth * state[1]
    flux_north = column_depth * state[2]
    height, wind_east, wind_north = (state[0], state[1], state[2])
    rate_height = -(slope_east(flux_east) + slope_north(flux_north))
    rate_east = -(wind_east * slope_east(wind_east) + wind_north * slope_north(wind_east)) + CORIOLIS * wind_north - GRAVITY * slope_east(height)
    rate_north = -(wind_east * slope_east(wind_north) + wind_north * slope_north(wind_north)) - CORIOLIS * wind_east - GRAVITY * slope_north(height)
    return jnp.stack([rate_height, rate_east, rate_north])

def heun(state):
    first = state + TIME_STEP * tendency(state)
    return 0.5 * (state + first + TIME_STEP * tendency(first))

def restrict(field):
    fields, rows, cols = field.shape
    return field.reshape(fields, rows // RATIO, RATIO, cols // RATIO, RATIO).mean(axis=(2, 4))

def prolong(field):
    return jnp.repeat(jnp.repeat(field, RATIO, axis=-2), RATIO, axis=-1)

def wavenumbers(count, offset):
    index = offset + jnp.arange(count, dtype=jnp.int32)
    half = NC // 2
    shifted = jnp.where(index < half, index, index - NC)
    shifted = jnp.where(index == half, 0, shifted)
    return shifted.astype(jnp.float32) * (2.0 * math.pi / (NC * RATIO))

def apply_operator(real_part, imag_part, wave_east, wave_north):
    mixed_real = wave_east * real_part[1] + wave_north * real_part[2]
    mixed_imag = wave_east * imag_part[1] + wave_north * imag_part[2]
    height_real = MEAN_DEPTH * mixed_imag
    height_imag = -MEAN_DEPTH * mixed_real
    east_real = GRAVITY * wave_east * imag_part[0] + CORIOLIS * real_part[2]
    east_imag = -GRAVITY * wave_east * real_part[0] + CORIOLIS * imag_part[2]
    north_real = GRAVITY * wave_north * imag_part[0] - CORIOLIS * real_part[1]
    north_imag = -GRAVITY * wave_north * real_part[0] - CORIOLIS * imag_part[1]
    return (jnp.stack([height_real, east_real, north_real]), jnp.stack([height_imag, east_imag, north_imag]))

def propagate(spectra, wave_east, wave_north, slices):
    duration = slices * (STEPS * TIME_STEP)
    omega = jnp.sqrt(CORIOLIS * CORIOLIS + GRAVITY * MEAN_DEPTH * (wave_east * wave_east + wave_north * wave_north))
    sine_term = jnp.sin(omega * duration) / omega
    versine_term = (1.0 - jnp.cos(omega * duration)) / (omega * omega)
    once_real, once_imag = apply_operator(spectra[0], spectra[1], wave_east, wave_north)
    twice_real, twice_imag = apply_operator(once_real, once_imag, wave_east, wave_north)
    return jnp.stack([spectra[0] + sine_term * once_real + versine_term * twice_real, spectra[1] + sine_term * once_imag + versine_term * twice_imag])

def spectrum(field):
    transformed = jnp.fft.fft2(field)
    return jnp.stack([jnp.real(transformed), jnp.imag(transformed)])

def reference(start_old, incoming):
    wave_east = wavenumbers(NC, 0)[None, :]
    wave_north = wavenumbers(NC, 0)[:, None]
    carried = jnp.zeros((2, 3, NC, NC), jnp.float32)
    results = []
    for slice_index in range(SLICES):
        fine = start_old[slice_index]
        for step_index in range(STEPS):
            fine = heun(fine)
        coarse_fine = restrict(fine)
        drift = restrict(start_old[slice_index])
        if slice_index == 0:
            drift = drift - incoming
        forcing = spectrum(coarse_fine) - propagate(spectrum(drift), wave_east, wave_north, 1.0)
        carried = propagate(carried, wave_east, wave_north, 1.0) + forcing
        coarse_new = jnp.real(jnp.fft.ifft2(lax.complex(carried[0], carried[1])))
        results.append(fine + prolong(coarse_new - coarse_fine))
    return jnp.stack(results)
```

```python
import functools
import math

import jax
import jax.numpy as jnp
import numpy as np
from jax import lax
from jax.experimental import pallas as pl
from jax.experimental.pallas import tpu as pltpu
from jax.sharding import PartitionSpec as P

RATIO = 2
STEPS = 2
TIME_STEP = 0.25
CORIOLIS = 0.5
HALO = 8
CORES = 2
MESH = pl.DeviceIdType.MESH


def halves(table):
    high = table.astype(jnp.bfloat16)
    return high, (table - high.astype(np.float32)).astype(jnp.bfloat16)


def split(a):
    high = a.astype(jnp.bfloat16)
    return high, (a - high.astype(jnp.float32)).astype(jnp.bfloat16)


def dot(a, b, sides=(1, 0)):
    dims = (((sides[0],), (sides[1],)), ((), ()))
    return lax.dot_general(a, b, dims, preferred_element_type=jnp.float32)


def tables(nc, parts):
    half, rows = nc // 2, nc // parts
    x = np.arange(nc)
    angle = 2.0 * math.pi / nc * (np.outer(np.arange(half), x) % nc)
    real, imag = np.cos(angle), -np.sin(angle)
    imag[0] = (-1.0) ** x
    forward = np.stack([real, imag])
    wide = 0.5 * np.repeat(forward, RATIO, axis=2)

    angle = 2.0 * math.pi / nc * (np.outer(x, x) % nc)
    cos, sin = np.cos(angle), np.sin(angle)
    along = np.stack([np.stack([cos, -sin], 1), np.stack([sin, cos], 1)])
    back = np.stack([np.stack([cos, sin], 1), np.stack([-sin, cos], 1)])
    along = along.reshape(2, parts, rows, 2 * nc).transpose(1, 0, 2, 3).reshape(2 * nc, 2 * nc)
    back = back.reshape(2 * nc, 2, parts, rows).transpose(0, 2, 1, 3).reshape(2 * nc, 2 * nc)

    scale = np.full((1, half, 1), 2.0 / (nc * nc))
    scale[:, 0] = 1.0 / (nc * nc)
    inverse = np.repeat(forward * scale, RATIO, axis=2).reshape(nc, -1)

    index = np.where(x < half, x, x - nc)
    index = np.where(x == half, 0, index)
    wave = index * (2.0 * math.pi / (nc * RATIO))
    omega = np.sqrt(CORIOLIS**2 + wave[:half, None] ** 2 + wave[None, :] ** 2)
    duration = STEPS * TIME_STEP
    sine = np.sin(omega * duration) / omega
    versine = (1.0 - np.cos(omega * duration)) / omega**2
    single = lambda a: np.asarray(a, np.float32)
    return [single(a) for a in (forward, wide, along, back, inverse, wave, sine, versine)]


def tendency(window):
    width = window[0].shape[-1]
    mid = [a[8:16] for a in window]
    south = [a[7:15] for a in window]
    north = [a[9:17] for a in window]
    west = [pltpu.roll(a, 1, 1) for a in mid]
    east = [pltpu.roll(a, width - 1, 1) for a in mid]
    _, u, v = mid
    flux = (1.0 + east[0]) * east[1] - (1.0 + west[0]) * west[1]
    flux = flux + ((1.0 + north[0]) * north[2] - (1.0 + south[0]) * south[2])
    half_u, half_v = 0.5 * u, 0.5 * v
    rate_u = CORIOLIS * v - (
        half_u * (east[1] - west[1]) + half_v * (north[1] - south[1]) + 0.5 * (east[0] - west[0])
    )
    rate_v = -(CORIOLIS * u) - (
        half_u * (east[2] - west[2]) + half_v * (north[2] - south[2]) + 0.5 * (north[0] - south[0])
    )
    return mid, (-0.5 * flux, rate_u, rate_v)


def rows_at(row):
    return row if isinstance(row, int) else pl.multiple_of(row, 8)


def heun(rows, width, now, first):
    blocks = (rows + 2 * HALO) // 8
    pad = jnp.zeros((HALO, width), jnp.float32)

    def clear():
        for f in range(3):
            for ref in (now, first):
                ref[f, 0:8] = pad
                ref[f, 24 + rows : 32 + rows] = pad

    def window(ref, block):
        at = rows_at(block * 8)
        return [ref[f, pl.ds(at, 24)] for f in range(3)]

    def predict(block, _):
        mid, rate = tendency(window(now, block))
        at = rows_at(block * 8 + 8)
        for f in range(3):
            first[f, pl.ds(at, 8)] = mid[f] + TIME_STEP * rate[f]
        return 0

    def correct(out, shift):
        def body(block, _):
            mid, rate = tendency(window(first, block))
            at = rows_at(block * 8 + 8)
            to = rows_at(block * 8 + 8 - shift)
            for f in range(3):
                out[f, pl.ds(to, 8)] = 0.5 * (now[f, pl.ds(at, 8)] + mid[f] + TIME_STEP * rate[f])
            return 0

        return body

    def inner():
        clear()
        lax.fori_loop(2, blocks - 2, predict, 0)

    def edges():
        for block in (0, 1, blocks - 2, blocks - 1):
            predict(block, 0)
        lax.fori_loop(0, blocks, correct(now, 0), 0)

    def last(fine):
        lax.fori_loop(0, blocks, predict, 0)
        lax.fori_loop(1, blocks - 1, correct(fine, 16), 0)

    return inner, edges, last


def apply_operator(s, a, b):
    (hr, hi), (ur, ui), (vr, vi) = s
    return (
        (a * ui + b * vi, -(a * ur + b * vr)),
        (a * hi + CORIOLIS * vr, CORIOLIS * vi - a * hr),
        (b * hi - CORIOLIS * ur, -(b * hr) - CORIOLIS * ui),
    )


def kernel(
    size, state, incoming_far, pairs_far, twice_far, north_far,
    wide_h_far, wide_l_far, short_h_far, short_l_far, along_h, along_l, back_h, back_l, inverse_h, inverse_l,
    east_far, sine_far, versine_far, out,
    incoming, pairs, twice, north, now, first, fine, gap, mine, theirs, landed, arrived, acc, kept, relayed, change,
    leaving, going, returned, east, sine, versine,
    wide_h, wide_l, short_h, short_l, ah, al, bh, bl, ih, il,
    fetch, store, rim_send, rim_recv, t_send, t_recv, d_send, d_recv, e_send, e_recv, g_send, g_recv, h_send, h_recv,
):
    fields, rows, nc = incoming_far.shape
    wide_rows, width = state.shape[1:]
    half = nc // 2
    count = half // size
    each = count // CORES
    me, slot = lax.axis_index("space"), lax.axis_index("tm")
    peers = [lax.rem(me + d, size) for d in range(size)]
    origins = [lax.rem(me + size - d, size) for d in range(size)]

    share = pl.ds(pl.multiple_of(me * count, count), count)
    fetches = [
        pltpu.make_async_copy(source, target, fetch.at[n])
        for n, (source, target) in enumerate(
            (
                (state, now.at[:, pl.ds(16, wide_rows)]),
                (pairs_far, pairs),
                (wide_h_far, wide_h),
                (wide_l_far, wide_l),
                (incoming_far, incoming),
                (short_h_far, short_h),
                (short_l_far, short_l),
                (along_h, ah),
                (along_l, al),
                (east_far.at[share], east),
                (sine_far.at[share], sine),
                (versine_far.at[share], versine),
                (north_far, north),
                (back_h, bh),
                (back_l, bl),
                (twice_far, twice),
                (inverse_h, ih),
                (inverse_l, il),
            )
        )
    ]
    barrier = pltpu.get_barrier_semaphore()
    for d, peer in enumerate(peers):
        for core in range(CORES):
            if d > 0:
                pl.semaphore_signal(barrier, inc=1, device_id={"space": peer, "tm": core}, device_id_type=MESH)
    pl.semaphore_signal(barrier, inc=1, device_id={"tm": 1 - slot}, device_id_type=MESH)
    for copy in fetches:
        copy.start()

    def send(source, target, sender, receiver, peer, core):
        return pltpu.make_async_remote_copy(
            src_ref=source, dst_ref=target, send_sem=sender, recv_sem=receiver,
            device_id={"space": peer, "tm": core}, device_id_type=MESH,
        )

    rims = [
        send(
            state.at[:, pl.ds(source, HALO)], now.at[:, pl.ds(target, HALO)],
            rim_send.at[n], rim_recv.at[n], peer, slot,
        )
        for n, (source, target, peer) in enumerate(
            ((wide_rows - HALO, 8, peers[1]), (0, 16 + wide_rows, peers[-1]))
        )
    ]
    early = [send(gap.at[p], landed.at[me], d_send.at[n], d_recv.at[n], p, 1) for n, p in enumerate(peers)]
    ahead = send(gap, theirs, t_send.at[0], t_recv.at[0], me, 0)
    relay = send(kept.at[0], relayed, t_send.at[1], t_recv.at[1], me, 0)
    back = [send(leaving.at[p], returned.at[me], e_send.at[n], e_recv.at[n], p, 0) for n, p in enumerate(peers)]
    late = [
        [send(mine.at[p, c], arrived.at[me], g_send.at[n, c], g_recv.at[n], p, c) for c in range(CORES)]
        for n, p in enumerate(peers)
    ]
    home = [
        send(going.at[p], returned.at[me, slot], h_send.at[n], h_recv.at[n, slot], p, 1)
        for n, p in enumerate(peers)
    ]
    homes = [
        [send(going.at[p], returned.at[me, c], h_send.at[n], h_recv.at[n, c], p, 1) for c in range(CORES)]
        for n, p in enumerate(peers)
    ]

    def spectra_of(stacked, high, low):
        up, down = split(stacked)
        return dot(high, up, (1, 1)) + (dot(high, down, (1, 1)) + dot(low, up, (1, 1)))

    def x_spectra(ref):
        parts = [split(ref[f]) for f in range(fields)]
        averaged = [dot(pairs[...], up) + dot(pairs[...], down) for up, down in parts]
        return spectra_of(jnp.concatenate(averaged, 0), wide_h[...], wide_l[...])

    def lay_out(value, put):
        for f in range(fields):
            both = value[:, f * rows : (f + 1) * rows]
            both = jnp.concatenate([both[:half], both[half:]], 1)
            for j in range(size):
                for c in range(CORES):
                    at = (j * CORES + c) * each
                    put((j, c, f), both[at : at + each])

    pl.semaphore_wait(barrier, CORES * size - 1)
    for copy in rims:
        copy.start()

    for copy in fetches[:4]:
        copy.wait()

    def put_gap(at, value):
        gap[at] = -value

    def add_gap(at, value):
        gap[at] += value

    def put_mine(at, value):
        mine[at] = theirs[at] + value

    lay_out(x_spectra(now.at[:, pl.ds(16, wide_rows)]), put_gap)
    for copy in fetches[4:7]:
        copy.wait()

    @pl.when(slot == 0)
    def _():
        fresh = jnp.concatenate([incoming[f] for f in range(fields)], 0)
        lay_out(spectra_of(fresh, short_h[...], short_l[...]), add_gap)
        for copy in early:
            copy.start()

    @pl.when(slot == 1)
    def _():
        ahead.start()

    inner, edges, last = heun(wide_rows, width, now, first)
    inner()
    for copy in rims:
        copy.wait()
    edges()

    def y_spectra(blocks):
        up, down = split(jnp.concatenate(blocks, 1))
        return dot(up, ah[...]) + (dot(down, ah[...]) + dot(up, al[...]))

    def y_fields(value):
        up, down = split(value)
        return dot(up, bh[...]) + (dot(down, bh[...]) + dot(up, bl[...]))

    def propagate(source, target, core):
        tile = min(each, 8)
        for r in range(0, each, tile):
            at = pl.ds(core * each + r, tile)
            wave = slice(r, r + tile)
            spectra = [(source[f, wave, :nc], source[f, wave, nc:]) for f in range(fields)]
            once = apply_operator(spectra, east[at], north[:tile])
            twofold = apply_operator(once, east[at], north[:tile])
            for f in range(fields):
                for part, lanes in enumerate((slice(0, nc), slice(nc, 2 * nc))):
                    target[f, wave, lanes] = (
                        spectra[f][part] + sine[at] * once[f][part] + versine[at] * twofold[f][part]
                    )

    for copy in fetches[7:]:
        copy.wait()

    @pl.when(slot == 1)
    def _():
        for copy in early:
            copy.wait_recv()
        order = [(c, f) for c in range(CORES) for f in range(fields)]
        value = y_spectra(
            [jnp.concatenate([landed[j, c, f] for c, f in order], 0) for j in range(size)]
        )
        for n, (c, f) in enumerate(order):
            acc[c, f] = value[n * each : (n + 1) * each]
        for c in range(CORES):
            propagate(acc.at[c], kept.at[c], c)
        relay.start()
        value = y_fields(jnp.concatenate([kept[c, f] for c, f in order], 0))
        for j in range(size):
            for n, (c, f) in enumerate(order):
                leaving[j, c, f] = value[n * each : (n + 1) * each, j * 2 * rows : (j + 1) * 2 * rows]
        for copy in back:
            copy.start()

    last(fine)

    @pl.when(slot == 0)
    def _():
        for copy in early:
            copy.wait_send()
        ahead.wait_recv()
        lay_out(x_spectra(fine), put_mine)
        for n in range(size):
            for c in range(CORES):
                if n > 0 or c > 0:
                    late[n][c].start()
        arrived[me] = mine[me, 0]
        relay.wait_recv()

    @pl.when(slot == 1)
    def _():
        relay.wait_send()
        relayed[...] = kept[1]
        late[0][1].wait_recv()

    for n in range(1, size):
        late[n][0].wait_recv()
    value = y_spectra([jnp.concatenate([arrived[j, f] for f in range(fields)], 0) for j in range(size)])
    for f in range(fields):
        acc[0, f] = value[f * each : (f + 1) * each] + relayed[f]

    propagate_at(propagate, acc, change, slot)
    value = y_fields(jnp.concatenate([change[f] for f in range(fields)], 0))
    for j in range(size):
        for f in range(fields):
            going[j, f] = value[f * each : (f + 1) * each, j * 2 * rows : (j + 1) * 2 * rows]
    for copy in home[1:]:
        copy.start()

    @pl.when(slot == 0)
    def _():
        home[0].start()
        for n in range(size):
            for c in range(CORES):
                if n > 0 or c > 0:
                    late[n][c].wait_send()
        for copy in back:
            copy.wait_recv()

    @pl.when(slot == 1)
    def _():
        returned[me, 1] = going[me]
        ahead.wait_send()
        for copy in back:
            copy.wait_send()
        homes[0][0].wait_recv()
        for n in range(1, size):
            for c in range(CORES):
                homes[n][c].wait_recv()

    stores = []
    for f in range(fields):
        spectrum = jnp.concatenate([returned[j, c, f] for j in range(size) for c in range(CORES)], 0)
        up, down = (
            jnp.concatenate([dot(twice[c], part, (1, 1)) for c in range(2)], 1).astype(jnp.bfloat16)
            for part in split(spectrum)
        )
        fine[f] += dot(up, ih[...]) + (dot(down, ih[...]) + dot(up, il[...]))
        stores.append(pltpu.make_async_copy(fine.at[f], out.at[f], store.at[f]))
        stores[-1].start()

    for copy in home[1:]:
        copy.wait_send()

    @pl.when(slot == 0)
    def _():
        home[0].wait_send()

    for copy in stores:
        copy.wait()


def propagate_at(propagate, acc, change, slot):
    for core in range(CORES):
        @pl.when(slot == core)
        def _():
            propagate(acc.at[0], change, core)


def shards(start_old, incoming):
    size = lax.axis_size("space")
    state = start_old[0]
    width = state.shape[2]
    fields, rows, nc = incoming.shape
    half = nc // 2
    count = half // size
    each = count // CORES
    forward, wide, along, back, inverse, wave, sine, versine = tables(nc, size)
    pairs = np.repeat(np.eye(rows, dtype=np.float32), RATIO, axis=1)
    twice = np.zeros((2, RATIO * rows, 2 * rows), np.float32)
    twice[0, :, :rows] = twice[1, :, rows:] = pairs.T

    flat = lambda table: halves(table.reshape(nc, -1))
    east = np.repeat(wave[:half, None], nc, axis=1)
    north = np.repeat(wave[None, :], 8, axis=0)
    operands = [state, incoming, (0.5 * pairs).astype(jnp.bfloat16), twice.astype(jnp.bfloat16), north]
    distant = [*flat(wide), *flat(forward), *halves(along), *halves(back), *halves(inverse)]
    padded = (fields, state.shape[1] + 4 * HALO, width)
    blocks = (size, CORES, fields, each, 2 * rows)
    single = (size, fields, each, 2 * rows)
    whole = (fields, each, 2 * nc)
    shapes = [north.shape, padded, padded, state.shape]
    shapes += [blocks] * 4 + [single] + [(CORES, *whole)] * 2 + [whole] * 2
    shapes += [blocks, single, blocks] + [(count, nc)] * 3
    buffers = [pltpu.VMEM(incoming.shape, jnp.float32)]
    buffers += [pltpu.VMEM(table.shape, jnp.bfloat16) for table in operands[2:4]]
    buffers += [pltpu.VMEM(shape, jnp.float32) for shape in shapes]
    far = pl.BlockSpec(memory_space=pltpu.HBM)
    inputs = len(operands) + len(distant) + 3
    dma = pltpu.SemaphoreType.DMA
    result = pl.pallas_call(
        functools.partial(kernel, size),
        out_shape=jax.ShapeDtypeStruct(state.shape, jnp.float32),
        in_specs=[far] * inputs,
        out_specs=far,
        scratch_shapes=buffers
        + [pltpu.VMEM(table.shape, jnp.bfloat16) for table in distant]
        + [dma((inputs,)), dma((fields,))]
        + [dma((2,))] * 4
        + [dma((size,))] * 4
        + [dma((size, CORES)), dma((size,)), dma((size,)), dma((size, CORES))],
        compiler_params=pltpu.CompilerParams(
            collective_id=0, has_side_effects=True, vmem_limit_bytes=(64 << 20) - (128 << 10)
        ),
        cost_estimate=pl.CostEstimate(
            flops=40 * fields * count * nc * nc, bytes_accessed=32 * nc * nc, transcendentals=0
        ),
    )(*operands, *distant, east, sine, versine)
    return result[None]


def solution(mesh):
    placed = (P(("group", "tm"), None, "space", None), P("group", "space", None))
    return jax.shard_map(
        shards,
        mesh=mesh,
        in_specs=placed,
        out_specs=P(("group", "tm"), None, "space", None),
        check_vma=False,
    )
```

```python
import functools
import math

import jax
import jax.numpy as jnp
import numpy as np
from jax import lax
from jax.experimental import pallas as pl
from jax.experimental.pallas import tpu as pltpu
from jax.sharding import PartitionSpec as P

RATIO = 2
STEPS = 2
TIME_STEP = 0.25
CORIOLIS = 0.5
HALO = 8
RIM = 4
CORES = 2
LANES = 128
MESH = pl.DeviceIdType.MESH


def halves(table):
    high = table.astype(jnp.bfloat16)
    return high, (table - high.astype(np.float32)).astype(jnp.bfloat16)


def split(a):
    high = a.astype(jnp.bfloat16)
    return high, (a - high.astype(jnp.float32)).astype(jnp.bfloat16)


def dot(a, b, sides=(1, 0)):
    dims = (((sides[0],), (sides[1],)), ((), ()))
    return lax.dot_general(a, b, dims, preferred_element_type=jnp.float32)


def dot_split(a, high, low):
    up, down = split(a)
    count = a.shape[0]
    both = dot(jnp.concatenate([up, down], 0), high)
    return both[:count] + (both[count:] + dot(up, low))


def dot_table(high, low, a):
    up, down = split(a)
    count = a.shape[0]
    both = dot(high, jnp.concatenate([up, down], 0), (1, 1))
    return both[:, :count] + (both[:, count:] + dot(low, up, (1, 1)))


def tables(nc):
    half = nc // 2
    order = np.concatenate([np.arange(0, half, 2), np.arange(1, half, 2)])
    angle = 2.0 * math.pi / nc * (np.outer(order, np.arange(half)) % nc)
    real, imag = np.cos(angle), -np.sin(angle)
    imag[0] = (-1.0) ** np.arange(half)
    scale = np.full((half, 1), 2.0 / (nc * nc))
    scale[0] = 1.0 / (nc * nc)
    halved = lambda a: a.reshape(2, half // 2, half)
    forward = np.stack([halved(real), halved(imag)], 1).reshape(2, half, half)
    inverse = np.stack([halved(real * scale), halved(imag * scale)], 1).reshape(2, half, half)
    wide = np.repeat(forward / RATIO**2, RATIO, axis=2)
    inverse = np.repeat(inverse, RATIO, axis=2)

    y = np.arange(half)
    angle = 2.0 * math.pi / half * (np.outer(y, y) % half)
    turn = np.concatenate([np.cos(angle), np.sin(angle)], 1)
    angle = 2.0 * math.pi / nc * y
    twiddle = np.repeat(np.stack([np.cos(angle), -np.sin(angle)])[:, None], 8, axis=1)

    index = np.arange(nc)
    index = np.where(index < half, index, index - nc)
    index = np.where(index == -half, 0, index)
    wave = index * (2.0 * math.pi / (nc * RATIO))
    east = wave[order]
    north = np.concatenate([wave[0::2], wave[1::2]])
    omega = np.sqrt(CORIOLIS**2 + east[:, None] ** 2 + north[None, :] ** 2)
    duration = STEPS * TIME_STEP
    sine = np.sin(omega * duration) / omega
    versine = (1.0 - np.cos(omega * duration)) / omega**2
    single = lambda a: np.asarray(a, np.float32)
    return [single(a) for a in (forward, wide, turn, twiddle, inverse, east, north, sine, versine)]


def slopes(ref, at):
    blocks, lanes = ref.shape[1], ref.shape[3]
    lane = lax.broadcasted_iota(jnp.int32, (8, lanes), 1)
    begin, end = lane == 0, lane == lanes - 1
    mids = [[None] * blocks for _ in range(3)]
    rights = [[None] * blocks for _ in range(3)]
    lefts = [[None] * blocks for _ in range(3)]

    def mid(f, n):
        if mids[f][n] is None:
            mids[f][n] = ref[f, n, pl.ds(at, 8)]
        return mids[f][n]

    def right(f, n):
        if rights[f][n] is None:
            rights[f][n] = pltpu.roll(mid(f, n), 1, 1)
        return rights[f][n]

    def left(f, n):
        if lefts[f][n] is None:
            lefts[f][n] = pltpu.roll(mid(f, n), lanes - 1, 1)
        return lefts[f][n]

    for n in range(blocks):
        before, after = (n - 1) % blocks, (n + 1) % blocks
        hw, uw, vw = (jnp.where(begin, right(f, before), right(f, n)) for f in range(3))
        he, ue, ve = (jnp.where(end, left(f, after), left(f, n)) for f in range(3))
        hs, us, vs = (ref[f, n, pl.ds(at - 1, 8)] for f in range(3))
        hn, un, vn = (ref[f, n, pl.ds(at + 1, 8)] for f in range(3))
        h, u, v = (mid(f, n) for f in range(3))
        ux, vy = ue - uw, vn - vs
        rate_h = (ux + (he * ue - hw * uw)) + (vy + (hn * vn - hs * vs))
        rate_u = (u * ux + v * (un - us)) + ((he - hw) - v)
        rate_v = (u * (ve - vw) + v * vy) + ((hn - hs) + u)
        yield n, (h, u, v), (rate_h, rate_u, rate_v)


def heun(rows, now, first):
    blocks = (rows + 2 * HALO) // 8
    unit = 0.5 * TIME_STEP

    def rows_at(block):
        return block * 8 if isinstance(block, int) else pl.multiple_of(block * 8, 8)

    def predict(block, _):
        at = rows_at(block + 1)
        for n, mid, rate in slopes(now, at):
            for f in range(3):
                first[f, n, pl.ds(at, 8)] = mid[f] - unit * rate[f]
        return 0

    def correct(out, shift):
        def body(block, _):
            at, to = rows_at(block + 1), rows_at(block + 1 - shift)
            for n, mid, rate in slopes(first, at):
                for f in range(3):
                    out[f, n, pl.ds(to, 8)] = (
                        0.5 * (now[f, n, pl.ds(at, 8)] + mid[f]) - (0.5 * unit) * rate[f]
                    )
            return 0

        return body

    def inner():
        lax.fori_loop(2, blocks - 2, predict, 0)

    def edges():
        def edge(n, _):
            predict(jnp.where(n < 2, n, n + blocks - 4), 0)
            return 0

        lax.fori_loop(0, 4, edge, 0)
        lax.fori_loop(0, blocks, correct(now, 0), 0)

    def last(fine):
        lax.fori_loop(0, blocks, predict, 0)
        lax.fori_loop(1, blocks - 1, correct(fine, 2), 0)

    return inner, edges, last


def apply_operator(s, a, b):
    (hr, hi), (ur, ui), (vr, vi) = s
    return (
        (a * ui + b * vi, -(a * ur + b * vr)),
        (a * hi + CORIOLIS * vr, CORIOLIS * vi - a * hr),
        (b * hi - CORIOLIS * ur, -(b * hr) - CORIOLIS * ui),
    )


def kernel(
    size, state, incoming_far, mirror_far, north_far, twiddle_far,
    wide_h_far, wide_l_far, short_h_far, short_l_far, turn_h, turn_l, inverse_h, inverse_l,
    east_far, sine_far, versine_far, out,
    incoming, mirror, north, twiddle, rim_in, now, first, fine, gap, mine, theirs, landed, arrived, acc, kept, relayed, change,
    leaving, going, returned, east, sine, versine,
    wide_h, wide_l, short_h, short_l, th, tl, ih, il,
    fetch, store, rim_send, rim_recv, t_send, t_recv, d_send, d_recv, e_send, e_recv, g_send, g_recv, h_send, h_recv,
):
    fields, rows, nc = incoming_far.shape
    wide_rows, width = state.shape[1:]
    strips, lanes = now.shape[1], now.shape[3]
    half = nc // 2
    count = half // size
    each = count // CORES
    me, slot = lax.axis_index("space"), lax.axis_index("tm")
    peers = [lax.rem(me + d, size) for d in range(size)]
    origins = [lax.rem(me + size - d, size) for d in range(size)]

    share = pl.ds(pl.multiple_of(me * count, count), count)
    fetches = [
        pltpu.make_async_copy(source, target, fetch.at[n])
        for n, (source, target) in enumerate(
            (
                *(
                    (state.at[:, :, pl.ds(n * lanes, lanes)], now.at[:, n, pl.ds(2 * HALO, wide_rows)])
                    for n in range(strips)
                ),
                (wide_h_far, wide_h),
                (wide_l_far, wide_l),
                (incoming_far, incoming),
                (short_h_far, short_h),
                (short_l_far, short_l),
                (turn_h, th),
                (turn_l, tl),
                (twiddle_far, twiddle),
                (north_far, north),
                (east_far.at[share], east),
                (sine_far.at[share], sine),
                (versine_far.at[share], versine),
                (mirror_far, mirror),
                (inverse_h, ih),
                (inverse_l, il),
            )
        )
    ]
    rim_in[...] = jnp.zeros_like(rim_in)
    pad = jnp.zeros((fields, strips, HALO, lanes), jnp.float32)
    for ref in (now, first):
        ref[:, :, :HALO] = pad
        ref[:, :, 3 * HALO + wide_rows :] = pad

    barrier = pltpu.get_barrier_semaphore()
    for d, peer in enumerate(peers):
        for core in range(CORES):
            if d > 0:
                pl.semaphore_signal(barrier, inc=1, device_id={"space": peer, "tm": core}, device_id_type=MESH)
    pl.semaphore_signal(barrier, inc=1, device_id={"tm": 1 - slot}, device_id_type=MESH)
    for copy in fetches[: strips + 5]:
        copy.start()

    def send(source, target, sender, receiver, peer, core):
        return pltpu.make_async_remote_copy(
            src_ref=source, dst_ref=target, send_sem=sender, recv_sem=receiver,
            device_id={"space": peer, "tm": core}, device_id_type=MESH,
        )

    rims = [
        send(
            state.at[:, pl.ds(source, RIM)], rim_in.at[n, :, pl.ds(target, RIM)],
            rim_send.at[n], rim_recv.at[n], peer, slot,
        )
        for n, (source, target, peer) in enumerate(
            ((wide_rows - RIM, HALO - RIM, peers[1]), (0, 0, peers[-1]))
        )
    ]
    early = [send(gap.at[p], landed.at[me], d_send.at[n], d_recv.at[n], p, 1) for n, p in enumerate(peers)]
    ahead = send(gap, theirs, t_send.at[0], t_recv.at[0], me, 0)
    relay = send(kept.at[0], relayed, t_send.at[1], t_recv.at[1], me, 0)
    back = [send(leaving.at[p], returned.at[me], e_send.at[n], e_recv.at[n], p, 0) for n, p in enumerate(peers)]
    late = [
        [send(mine.at[p, c], arrived.at[me], g_send.at[n, c], g_recv.at[n], p, c) for c in range(CORES)]
        for n, p in enumerate(peers)
    ]
    home = [
        send(going.at[p], returned.at[me, slot], h_send.at[n], h_recv.at[n, slot], p, 1)
        for n, p in enumerate(peers)
    ]
    homes = [
        [send(going.at[p], returned.at[me, c], h_send.at[n], h_recv.at[n, c], p, 1) for c in range(CORES)]
        for n, p in enumerate(peers)
    ]

    def x_spectra(value, high, low, put):
        middle = value.shape[1] // 2
        west, east_side = value[:, :middle], value[:, middle:]
        for parity, part in enumerate((west + east_side, west - east_side)):
            found = dot_table(high[parity], low[parity], part)
            for f in range(fields):
                both = found[:, f * rows : (f + 1) * rows]
                both = jnp.concatenate([both[: half // 2], both[half // 2 :]], 1)
                for n in range(size * CORES // 2):
                    j, c = divmod(parity * size * CORES // 2 + n, CORES)
                    put((j, c, f), both[n * each : (n + 1) * each])

    def paired(ref, start):
        parts = [
            jnp.concatenate(
                [
                    ref[f, n, pl.ds(start, rows, stride=2)] + ref[f, n, pl.ds(start + 1, rows, stride=2)]
                    for n in range(strips)
                ],
                1,
            )
            for f in range(fields)
        ]
        return jnp.concatenate(parts, 0)

    pl.semaphore_wait(barrier, CORES * size - 1)
    for copy in rims:
        copy.start()

    for copy in fetches[: strips + 2]:
        copy.wait()

    def put_gap(at, value):
        gap[at] = -value

    def add_gap(at, value):
        gap[at] += value

    def put_mine(at, value):
        mine[at] = theirs[at] + value

    x_spectra(paired(now, 16), wide_h, wide_l, put_gap)
    for copy in fetches[strips + 2 : strips + 5]:
        copy.wait()

    @pl.when(slot == 0)
    def _():
        fresh = jnp.concatenate([incoming[f] for f in range(fields)], 0)
        x_spectra(fresh, short_h, short_l, add_gap)
        for copy in early:
            copy.start()

    @pl.when(slot == 1)
    def _():
        ahead.start()

    for copy in fetches[strips + 5 :]:
        copy.start()

    inner, edges, last = heun(wide_rows, now, first)
    inner()
    for copy in rims:
        copy.wait()
    for n in range(strips):
        across = slice(n * lanes, (n + 1) * lanes)
        now[:, n, HALO : 2 * HALO] = rim_in[0, :, :, across]
        now[:, n, 2 * HALO + wide_rows : 3 * HALO + wide_rows] = rim_in[1, :, :, across]
    edges()

    def turned(parts, sign):
        length = parts[0].shape[0]
        found = dot_split(jnp.concatenate(parts, 0), th[...], tl[...])
        cos = [found[n * length : (n + 1) * length, :half] for n in range(4)]
        sin = [found[n * length : (n + 1) * length, half:] for n in range(4)]
        return [
            (cos[n] - sign * sin[n + 1], cos[n + 1] + sign * sin[n]) for n in (0, 2)
        ]

    def y_spectra(blocks):
        low, high = blocks[: size // 2], blocks[size // 2 :]
        both = [a + b for a, b in zip(low, high)]
        apart = [a - b for a, b in zip(low, high)]
        gather = lambda pieces, at: jnp.concatenate([a[:, at * rows : (at + 1) * rows] for a in pieces], 1)
        real, imag = gather(apart, 0), gather(apart, 1)
        a, b = twiddle[0, 0:1], twiddle[1, 0:1]
        (er, ei), (our, oi) = turned(
            [gather(both, 0), gather(both, 1), real * a - imag * b, real * b + imag * a], -1.0
        )
        return jnp.concatenate([er, our, ei, oi], 1)

    def y_fields(value):
        (er, ei), (our, oi) = turned([value[:, n * half : (n + 1) * half] for n in (0, 2, 1, 3)], 1.0)
        a, b = twiddle[0, 0:1], twiddle[1, 0:1]
        our, oi = our * a + oi * b, oi * a - our * b
        blocks = []
        for real, imag in ((er + our, ei + oi), (er - our, ei - oi)):
            for n in range(size // 2):
                at = slice(n * rows, (n + 1) * rows)
                blocks.append(jnp.concatenate([real[:, at], imag[:, at]], 1))
        return blocks

    def propagate(source, target, core):
        tile = min(each, 8)
        for r in range(0, each, tile):
            at = pl.ds(core * each + r, tile)
            wave = slice(r, r + tile)
            spectra = [(source[f, wave, :nc], source[f, wave, nc:]) for f in range(fields)]
            once = apply_operator(spectra, east[at], north[:tile])
            twofold = apply_operator(once, east[at], north[:tile])
            for f in range(fields):
                for part, lanes in enumerate((slice(0, nc), slice(nc, 2 * nc))):
                    target[f, wave, lanes] = (
                        spectra[f][part] + sine[at] * once[f][part] + versine[at] * twofold[f][part]
                    )

    for copy in fetches[strips + 5 :]:
        copy.wait()

    @pl.when(slot == 1)
    def _():
        for copy in early:
            copy.wait_recv()
        order = [(c, f) for c in range(CORES) for f in range(fields)]
        value = y_spectra(
            [jnp.concatenate([landed[j, c, f] for c, f in order], 0) for j in range(size)]
        )
        for n, (c, f) in enumerate(order):
            acc[c, f] = value[n * each : (n + 1) * each]
        for c in range(CORES):
            propagate(acc.at[c], kept.at[c], c)
        relay.start()
        value = y_fields(jnp.concatenate([kept[c, f] for c, f in order], 0))
        for j in range(size):
            for n, (c, f) in enumerate(order):
                leaving[j, c, f] = value[j][n * each : (n + 1) * each]
        for copy in back:
            copy.start()

    @pl.when(slot == 0)
    def _():
        last(fine)
        for copy in early:
            copy.wait_send()
        ahead.wait_recv()
        x_spectra(paired(fine, 0), wide_h, wide_l, put_mine)
        for n in range(size):
            for c in range(CORES):
                if n > 0 or c > 0:
                    late[n][c].start()
        arrived[me] = mine[me, 0]
        relay.wait_recv()

    @pl.when(slot == 1)
    def _():
        relay.wait_send()
        relayed[...] = kept[1]
        late[0][1].wait_recv()

    for n in range(1, size):
        late[n][0].wait_recv()
    value = y_spectra([jnp.concatenate([arrived[j, f] for f in range(fields)], 0) for j in range(size)])
    for f in range(fields):
        acc[0, f] = value[f * each : (f + 1) * each] + relayed[f]

    propagate_at(propagate, acc, change, slot)
    value = y_fields(jnp.concatenate([change[f] for f in range(fields)], 0))
    for j in range(size):
        for f in range(fields):
            going[j, f] = value[j][f * each : (f + 1) * each]
    for copy in home[1:]:
        copy.start()

    @pl.when(slot == 0)
    def _():
        home[0].start()
        for n in range(size):
            for c in range(CORES):
                if n > 0 or c > 0:
                    late[n][c].wait_send()
        for copy in back:
            copy.wait_recv()

    @pl.when(slot == 1)
    def _():
        returned[me, 1] = going[me]
        last(fine)
        ahead.wait_send()
        for copy in back:
            copy.wait_send()
        homes[0][0].wait_recv()
        for n in range(1, size):
            for c in range(CORES):
                homes[n][c].wait_recv()

    turned_up, turned_down = [], []
    for f in range(fields):
        spectrum = jnp.concatenate([returned[j, c, f] for j in range(size) for c in range(CORES)], 0)
        for part, parts in zip(split(spectrum), (turned_up, turned_down)):
            wide_part = dot(mirror[...], part, (1, 1)).astype(jnp.bfloat16)
            parts.append([wide_part[:rows], wide_part[rows:]])
    sums = []
    for parity in range(2):
        at = slice(parity * half // 2, (parity + 1) * half // 2)
        up, down = (
            jnp.concatenate([jnp.concatenate([real[:, at], imag[:, at]], 1) for real, imag in parts], 0)
            for parts in (turned_up, turned_down)
        )
        both = dot(jnp.concatenate([up, down], 0), ih[parity])
        sums.append(both[: up.shape[0]] + (both[up.shape[0] :] + dot(up, il[parity])))
    stores = []
    for n in range(strips):
        at = n % (strips // 2) * lanes
        even, odd = (a[:, at : at + lanes] for a in sums)
        change_n = even + odd if n < strips // 2 else even - odd
        for f in range(fields):
            for parity in range(RATIO):
                fine[f, n, pl.ds(parity, rows, stride=RATIO)] += change_n[f * rows : (f + 1) * rows]
        stores.append(
            pltpu.make_async_copy(fine.at[:, n], out.at[:, :, pl.ds(n * lanes, lanes)], store.at[n])
        )
        stores[-1].start()

    for copy in home[1:]:
        copy.wait_send()

    @pl.when(slot == 0)
    def _():
        home[0].wait_send()

    for copy in stores:
        copy.wait()


def propagate_at(propagate, acc, change, slot):
    for core in range(CORES):
        @pl.when(slot == core)
        def _():
            propagate(acc.at[0], change, core)


def shards(start_old, incoming):
    size = lax.axis_size("space")
    state = start_old[0]
    width = state.shape[2]
    fields, rows, nc = incoming.shape
    half = nc // 2
    count = half // size
    each = count // CORES
    forward, wide, turn, twiddle, inverse, east, north, sine, versine = tables(nc)
    mirror = np.eye(2 * rows, dtype=np.float32)
    east = np.repeat(east[:, None], nc, axis=1)
    north = np.repeat(north[None, :], 8, axis=0)
    operands = [state, incoming, mirror.astype(jnp.bfloat16), north, twiddle]
    distant = [*halves(wide), *halves(forward), *halves(turn), *halves(inverse)]
    strips = width // LANES
    padded = (fields, strips, state.shape[1] + 4 * HALO, LANES)
    blocks = (size, CORES, fields, each, 2 * rows)
    single = (size, fields, each, 2 * rows)
    whole = (fields, each, 2 * nc)
    shapes = [north.shape, twiddle.shape, (2, fields, HALO, width), padded, padded]
    shapes += [(fields, strips, state.shape[1], LANES)]
    shapes += [blocks] * 4 + [single] + [(CORES, *whole)] * 2 + [whole] * 2
    shapes += [blocks, single, blocks] + [(count, nc)] * 3
    buffers = [pltpu.VMEM(incoming.shape, jnp.float32)]
    buffers += [pltpu.VMEM(mirror.shape, jnp.bfloat16)]
    buffers += [pltpu.VMEM(shape, jnp.float32) for shape in shapes]
    far = pl.BlockSpec(memory_space=pltpu.HBM)
    inputs = len(operands) + len(distant) + 3
    dma = pltpu.SemaphoreType.DMA
    result = pl.pallas_call(
        functools.partial(kernel, size),
        out_shape=jax.ShapeDtypeStruct(state.shape, jnp.float32),
        in_specs=[far] * inputs,
        out_specs=far,
        scratch_shapes=buffers
        + [pltpu.VMEM(table.shape, jnp.bfloat16) for table in distant]
        + [dma((inputs + strips,)), dma((strips,))]
        + [dma((2,))] * 4
        + [dma((size,))] * 4
        + [dma((size, CORES)), dma((size,)), dma((size,)), dma((size, CORES))],
        compiler_params=pltpu.CompilerParams(
            collective_id=0, has_side_effects=True, vmem_limit_bytes=(64 << 20) - (128 << 10)
        ),
        cost_estimate=pl.CostEstimate(
            flops=40 * fields * count * nc * nc, bytes_accessed=32 * nc * nc, transcendentals=0
        ),
    )(*operands, *distant, east, sine, versine)
    return result[None]


def solution(mesh):
    placed = (P(("group", "tm"), None, "space", None), P("group", "space", None))
    return jax.shard_map(
        shards,
        mesh=mesh,
        in_specs=placed,
        out_specs=P(("group", "tm"), None, "space", None),
        check_vma=False,
    )
```

```python
import functools
import math

import jax
import jax.numpy as jnp
import numpy as np
from jax import lax
from jax.experimental import pallas as pl
from jax.experimental.pallas import tpu as pltpu
from jax.sharding import PartitionSpec as P

RATIO = 2
STEPS = 2
TIME_STEP = 0.25
CORIOLIS = 0.5
HALO = 8
RIM = 4
CORES = 2
LANES = 128
MESH = pl.DeviceIdType.MESH


def halves(table):
    high = table.astype(jnp.bfloat16)
    return high, (table - high.astype(np.float32)).astype(jnp.bfloat16)


def split(a):
    high = a.astype(jnp.bfloat16)
    return high, (a - high.astype(jnp.float32)).astype(jnp.bfloat16)


def dot(a, b, sides=(1, 0)):
    dims = (((sides[0],), (sides[1],)), ((), ()))
    return lax.dot_general(a, b, dims, preferred_element_type=jnp.float32)


def dot_split(a, high, low):
    up, down = split(a)
    count = a.shape[0]
    both = dot(jnp.concatenate([up, down], 0), high)
    return both[:count] + (both[count:] + dot(up, low))


def dot_table(high, low, a):
    up, down = split(a)
    count = a.shape[0]
    both = dot(high, jnp.concatenate([up, down], 0), (1, 1))
    return both[:, :count] + (both[:, count:] + dot(low, up, (1, 1)))


def tables(nc):
    half = nc // 2
    order = np.concatenate([np.arange(0, half, 2), np.arange(1, half, 2)])
    angle = 2.0 * math.pi / nc * (np.outer(order, np.arange(half)) % nc)
    real, imag = np.cos(angle), -np.sin(angle)
    imag[0] = (-1.0) ** np.arange(half)
    scale = np.full((half, 1), 2.0 / (nc * nc))
    scale[0] = 1.0 / (nc * nc)
    halved = lambda a: a.reshape(2, half // 2, half)
    forward = np.stack([halved(real), halved(imag)], 1).reshape(2, half, half)
    inverse = np.stack([halved(real * scale), halved(imag * scale)], 1).reshape(2, half, half)
    wide = np.repeat(forward / RATIO**2, RATIO, axis=2)
    inverse = np.repeat(inverse, RATIO, axis=2)

    y = np.arange(half)
    angle = 2.0 * math.pi / half * (np.outer(y, y) % half)
    turn = np.concatenate([np.cos(angle), np.sin(angle)], 1)
    angle = 2.0 * math.pi / nc * y
    twiddle = np.repeat(np.stack([np.cos(angle), -np.sin(angle)])[:, None], 8, axis=1)

    index = np.arange(nc)
    index = np.where(index < half, index, index - nc)
    index = np.where(index == -half, 0, index)
    wave = index * (2.0 * math.pi / (nc * RATIO))
    east = wave[order]
    north = np.concatenate([wave[0::2], wave[1::2]])
    omega = np.sqrt(CORIOLIS**2 + east[:, None] ** 2 + north[None, :] ** 2)
    duration = STEPS * TIME_STEP
    sine = np.sin(omega * duration) / omega
    versine = (1.0 - np.cos(omega * duration)) / omega**2
    single = lambda a: np.asarray(a, np.float32)
    return [single(a) for a in (forward, wide, turn, twiddle, inverse, east, north, sine, versine)]


def slopes(ref, at):
    blocks, lanes = ref.shape[1], ref.shape[3]
    lane = lax.broadcasted_iota(jnp.int32, (8, lanes), 1)
    begin, end = lane == 0, lane == lanes - 1
    mids = [[None] * blocks for _ in range(3)]
    rights = [[None] * blocks for _ in range(3)]
    lefts = [[None] * blocks for _ in range(3)]

    def mid(f, n):
        if mids[f][n] is None:
            mids[f][n] = ref[f, n, pl.ds(at, 8)]
        return mids[f][n]

    def right(f, n):
        if rights[f][n] is None:
            rights[f][n] = pltpu.roll(mid(f, n), 1, 1)
        return rights[f][n]

    def left(f, n):
        if lefts[f][n] is None:
            lefts[f][n] = pltpu.roll(mid(f, n), lanes - 1, 1)
        return lefts[f][n]

    for n in range(blocks):
        before, after = (n - 1) % blocks, (n + 1) % blocks
        hw, uw, vw = (jnp.where(begin, right(f, before), right(f, n)) for f in range(3))
        he, ue, ve = (jnp.where(end, left(f, after), left(f, n)) for f in range(3))
        hs, us, vs = (ref[f, n, pl.ds(at - 1, 8)] for f in range(3))
        hn, un, vn = (ref[f, n, pl.ds(at + 1, 8)] for f in range(3))
        h, u, v = (mid(f, n) for f in range(3))
        ux, vy = ue - uw, vn - vs
        rate_h = (ux + (he * ue - hw * uw)) + (vy + (hn * vn - hs * vs))
        rate_u = (u * ux + v * (un - us)) + ((he - hw) - v)
        rate_v = (u * (ve - vw) + v * vy) + ((hn - hs) + u)
        yield n, (h, u, v), (rate_h, rate_u, rate_v)


def loop(start, stop, body):
    count = stop - start
    if count > 0:
        unroll = max(n for n in range(1, 9) if count % n == 0)
        lax.fori_loop(start, stop, lambda n, _: body(n), None, unroll=unroll)


def heun(rows, now, first, fine):
    blocks = (rows + 2 * HALO) // 8
    unit = 0.5 * TIME_STEP

    def rows_at(block):
        return pl.multiple_of(block * 8, 8)

    def predict(block):
        at = rows_at(block + 1)
        found = [(f, n, mid[f] - unit * rate[f]) for n, mid, rate in slopes(now, at) for f in range(3)]
        for f, n, value in found:
            first[f, n, pl.ds(at, 8)] = value

    def correct(out, shift):
        def body(block):
            at, to = rows_at(block + 1), rows_at(block + 1 - shift)
            found = [
                (f, n, 0.5 * (now[f, n, pl.ds(at, 8)] + mid[f]) - (0.5 * unit) * rate[f])
                for n, mid, rate in slopes(first, at)
                for f in range(3)
            ]
            for f, n, value in found:
                out[f, n, pl.ds(to, 8)] = value

        return body

    stages = [(predict, 0), (correct(now, 0), 0), (predict, 0), (correct(fine, 2), 1)]

    def inside():
        for depth, (body, _) in enumerate(stages):
            loop(2 + depth, blocks - 2 - depth, body)

    def outside():
        for depth, (body, begin) in enumerate(stages):
            low, high = 2 + depth, blocks - 2 - depth
            if low < high:
                side = low - begin
                skip = high - low
                loop(0, 2 * side, lambda n: body(jnp.where(n < side, n, n + skip) + begin))
            else:
                loop(begin, blocks - begin, body)

    return inside, outside


def apply_operator(s, a, b):
    (hr, hi), (ur, ui), (vr, vi) = s
    return (
        (a * ui + b * vi, -(a * ur + b * vr)),
        (a * hi + CORIOLIS * vr, CORIOLIS * vi - a * hr),
        (b * hi - CORIOLIS * ur, -(b * hr) - CORIOLIS * ui),
    )


def kernel(
    size, state, incoming_far, mirror_far, north_far, twiddle_far,
    wide_h_far, wide_l_far, short_h_far, short_l_far, turn_h, turn_l, inverse_h, inverse_l,
    east_far, sine_far, versine_far, out,
    incoming, mirror, north, twiddle, rim_in, now, first, fine, gap, mine, theirs, landed, arrived, acc, kept, relayed, change,
    leaving, going, returned, east, sine, versine,
    wide_h, wide_l, short_h, short_l, th, tl, ih, il,
    fetch, store, rim_send, rim_recv, t_send, t_recv, d_send, d_recv, e_send, e_recv, g_send, g_recv, h_send, h_recv,
):
    fields, rows, nc = incoming_far.shape
    wide_rows, width = state.shape[1:]
    strips, lanes = now.shape[1], now.shape[3]
    half = nc // 2
    count = half // size
    each = count // CORES
    me, slot = lax.axis_index("space"), lax.axis_index("tm")
    peers = [lax.rem(me + d, size) for d in range(size)]
    origins = [lax.rem(me + size - d, size) for d in range(size)]

    share = pl.ds(pl.multiple_of(me * count, count), count)
    fetches = [
        pltpu.make_async_copy(source, target, fetch.at[n])
        for n, (source, target) in enumerate(
            (
                *(
                    (state.at[:, :, pl.ds(n * lanes, lanes)], now.at[:, n, pl.ds(2 * HALO, wide_rows)])
                    for n in range(strips)
                ),
                (wide_h_far, wide_h),
                (wide_l_far, wide_l),
                (incoming_far, incoming),
                (short_h_far, short_h),
                (short_l_far, short_l),
                (turn_h, th),
                (turn_l, tl),
                (twiddle_far, twiddle),
                (north_far, north),
                (east_far.at[share], east),
                (sine_far.at[share], sine),
                (versine_far.at[share], versine),
                (mirror_far, mirror),
                (inverse_h, ih),
                (inverse_l, il),
            )
        )
    ]
    rim_in[...] = jnp.zeros_like(rim_in)
    pad = jnp.zeros((fields, strips, HALO, lanes), jnp.float32)
    for ref in (now, first):
        ref[:, :, :HALO] = pad
        ref[:, :, 3 * HALO + wide_rows :] = pad

    barrier = pltpu.get_barrier_semaphore()
    for d, peer in enumerate(peers):
        for core in range(CORES):
            if d > 0:
                pl.semaphore_signal(barrier, inc=1, device_id={"space": peer, "tm": core}, device_id_type=MESH)
    pl.semaphore_signal(barrier, inc=1, device_id={"tm": 1 - slot}, device_id_type=MESH)
    for copy in fetches[: strips + 5]:
        copy.start()

    def send(source, target, sender, receiver, peer, core):
        return pltpu.make_async_remote_copy(
            src_ref=source, dst_ref=target, send_sem=sender, recv_sem=receiver,
            device_id={"space": peer, "tm": core}, device_id_type=MESH,
        )

    rims = [
        send(
            state.at[:, pl.ds(source, RIM)], rim_in.at[n, :, pl.ds(target, RIM)],
            rim_send.at[n], rim_recv.at[n], peer, slot,
        )
        for n, (source, target, peer) in enumerate(
            ((wide_rows - RIM, HALO - RIM, peers[1]), (0, 0, peers[-1]))
        )
    ]
    early = [send(gap.at[p], landed.at[me], d_send.at[n], d_recv.at[n], p, 1) for n, p in enumerate(peers)]
    ahead = send(gap, theirs, t_send.at[0], t_recv.at[0], me, 0)
    relay = send(kept.at[0], relayed, t_send.at[1], t_recv.at[1], me, 0)
    back = [send(leaving.at[p], returned.at[me], e_send.at[n], e_recv.at[n], p, 0) for n, p in enumerate(peers)]
    late = [
        [send(mine.at[p, c], arrived.at[me], g_send.at[n, c], g_recv.at[n], p, c) for c in range(CORES)]
        for n, p in enumerate(peers)
    ]
    home = [
        send(going.at[p], returned.at[me, slot], h_send.at[n], h_recv.at[n, slot], p, 1)
        for n, p in enumerate(peers)
    ]
    homes = [
        [send(going.at[p], returned.at[me, c], h_send.at[n], h_recv.at[n, c], p, 1) for c in range(CORES)]
        for n, p in enumerate(peers)
    ]

    def x_spectra(value, high, low, put):
        middle = value.shape[1] // 2
        west, east_side = value[:, :middle], value[:, middle:]
        for parity, part in enumerate((west + east_side, west - east_side)):
            found = dot_table(high[parity], low[parity], part)
            for f in range(fields):
                both = found[:, f * rows : (f + 1) * rows]
                both = jnp.concatenate([both[: half // 2], both[half // 2 :]], 1)
                for n in range(size * CORES // 2):
                    j, c = divmod(parity * size * CORES // 2 + n, CORES)
                    put((j, c, f), both[n * each : (n + 1) * each])

    def paired(ref, start):
        parts = [
            jnp.concatenate(
                [
                    ref[f, n, pl.ds(start, rows, stride=2)] + ref[f, n, pl.ds(start + 1, rows, stride=2)]
                    for n in range(strips)
                ],
                1,
            )
            for f in range(fields)
        ]
        return jnp.concatenate(parts, 0)

    for copy in fetches[: strips + 2]:
        copy.wait()

    def put_gap(at, value):
        gap[at] = -value

    def add_gap(at, value):
        gap[at] += value

    def put_mine(at, value):
        mine[at] = theirs[at] + value

    x_spectra(paired(now, 16), wide_h, wide_l, put_gap)
    for copy in fetches[strips + 2 : strips + 5]:
        copy.wait()

    @pl.when(slot == 0)
    def _():
        fresh = jnp.concatenate([incoming[f] for f in range(fields)], 0)
        x_spectra(fresh, short_h, short_l, add_gap)

    pl.semaphore_wait(barrier, CORES * size - 1)
    for copy in rims:
        copy.start()

    @pl.when(slot == 0)
    def _():
        for copy in early:
            copy.start()

    @pl.when(slot == 1)
    def _():
        ahead.start()

    for copy in fetches[strips + 5 :]:
        copy.start()

    inside, outside = heun(wide_rows, now, first, fine)
    inside()
    for copy in rims:
        copy.wait()
    for n in range(strips):
        across = slice(n * lanes, (n + 1) * lanes)
        now[:, n, HALO : 2 * HALO] = rim_in[0, :, :, across]
        now[:, n, 2 * HALO + wide_rows : 3 * HALO + wide_rows] = rim_in[1, :, :, across]
    outside()

    def turned(parts, sign):
        length = parts[0].shape[0]
        found = dot_split(jnp.concatenate(parts, 0), th[...], tl[...])
        cos = [found[n * length : (n + 1) * length, :half] for n in range(4)]
        sin = [found[n * length : (n + 1) * length, half:] for n in range(4)]
        return [
            (cos[n] - sign * sin[n + 1], cos[n + 1] + sign * sin[n]) for n in (0, 2)
        ]

    def y_spectra(blocks):
        low, high = blocks[: size // 2], blocks[size // 2 :]
        both = [a + b for a, b in zip(low, high)]
        apart = [a - b for a, b in zip(low, high)]
        gather = lambda pieces, at: jnp.concatenate([a[:, at * rows : (at + 1) * rows] for a in pieces], 1)
        real, imag = gather(apart, 0), gather(apart, 1)
        a, b = twiddle[0, 0:1], twiddle[1, 0:1]
        (er, ei), (our, oi) = turned(
            [gather(both, 0), gather(both, 1), real * a - imag * b, real * b + imag * a], -1.0
        )
        return jnp.concatenate([er, our, ei, oi], 1)

    def y_fields(value):
        (er, ei), (our, oi) = turned([value[:, n * half : (n + 1) * half] for n in (0, 2, 1, 3)], 1.0)
        a, b = twiddle[0, 0:1], twiddle[1, 0:1]
        our, oi = our * a + oi * b, oi * a - our * b
        blocks = []
        for real, imag in ((er + our, ei + oi), (er - our, ei - oi)):
            for n in range(size // 2):
                at = slice(n * rows, (n + 1) * rows)
                blocks.append(jnp.concatenate([real[:, at], imag[:, at]], 1))
        return blocks

    def propagate(source, target, core):
        tile = min(each, 8)
        for r in range(0, each, tile):
            at = pl.ds(core * each + r, tile)
            wave = slice(r, r + tile)
            spectra = [(source[f, wave, :nc], source[f, wave, nc:]) for f in range(fields)]
            once = apply_operator(spectra, east[at], north[:tile])
            twofold = apply_operator(once, east[at], north[:tile])
            for f in range(fields):
                for part, lanes in enumerate((slice(0, nc), slice(nc, 2 * nc))):
                    target[f, wave, lanes] = (
                        spectra[f][part] + sine[at] * once[f][part] + versine[at] * twofold[f][part]
                    )

    for copy in fetches[strips + 5 :]:
        copy.wait()

    @pl.when(slot == 1)
    def _():
        for copy in early:
            copy.wait_recv()
        order = [(c, f) for c in range(CORES) for f in range(fields)]
        value = y_spectra(
            [jnp.concatenate([landed[j, c, f] for c, f in order], 0) for j in range(size)]
        )
        for n, (c, f) in enumerate(order):
            acc[c, f] = value[n * each : (n + 1) * each]
        for c in range(CORES):
            propagate(acc.at[c], kept.at[c], c)
        relay.start()
        value = y_fields(jnp.concatenate([kept[c, f] for c, f in order], 0))
        for j in range(size):
            for n, (c, f) in enumerate(order):
                leaving[j, c, f] = value[j][n * each : (n + 1) * each]
        for copy in back:
            copy.start()

    @pl.when(slot == 0)
    def _():
        for copy in early:
            copy.wait_send()
        ahead.wait_recv()
        x_spectra(paired(fine, 0), wide_h, wide_l, put_mine)
        for n in range(size):
            for c in range(CORES):
                if n > 0 or c > 0:
                    late[n][c].start()
        arrived[me] = mine[me, 0]
        relay.wait_recv()

    @pl.when(slot == 1)
    def _():
        relay.wait_send()
        relayed[...] = kept[1]
        late[0][1].wait_recv()

    for n in range(1, size):
        late[n][0].wait_recv()
    value = y_spectra([jnp.concatenate([arrived[j, f] for f in range(fields)], 0) for j in range(size)])
    for f in range(fields):
        acc[0, f] = value[f * each : (f + 1) * each] + relayed[f]

    propagate_at(propagate, acc, change, slot)
    value = y_fields(jnp.concatenate([change[f] for f in range(fields)], 0))
    for j in range(size):
        for f in range(fields):
            going[j, f] = value[j][f * each : (f + 1) * each]
    for copy in home[1:]:
        copy.start()

    @pl.when(slot == 0)
    def _():
        home[0].start()
        for n in range(size):
            for c in range(CORES):
                if n > 0 or c > 0:
                    late[n][c].wait_send()
        for copy in back:
            copy.wait_recv()

    @pl.when(slot == 1)
    def _():
        returned[me, 1] = going[me]
        ahead.wait_send()
        for copy in back:
            copy.wait_send()
        homes[0][0].wait_recv()
        for n in range(1, size):
            for c in range(CORES):
                homes[n][c].wait_recv()

    turned_up, turned_down = [], []
    for f in range(fields):
        spectrum = jnp.concatenate([returned[j, c, f] for j in range(size) for c in range(CORES)], 0)
        for part, parts in zip(split(spectrum), (turned_up, turned_down)):
            wide_part = dot(mirror[...], part, (1, 1)).astype(jnp.bfloat16)
            parts.append([wide_part[:rows], wide_part[rows:]])
    sums = []
    for parity in range(2):
        at = slice(parity * half // 2, (parity + 1) * half // 2)
        up, down = (
            jnp.concatenate([jnp.concatenate([real[:, at], imag[:, at]], 1) for real, imag in parts], 0)
            for parts in (turned_up, turned_down)
        )
        both = dot(jnp.concatenate([up, down], 0), ih[parity])
        sums.append(both[: up.shape[0]] + (both[up.shape[0] :] + dot(up, il[parity])))
    stores = []
    for n in range(strips):
        at = n % (strips // 2) * lanes
        even, odd = (a[:, at : at + lanes] for a in sums)
        change_n = even + odd if n < strips // 2 else even - odd
        for f in range(fields):
            for parity in range(RATIO):
                fine[f, n, pl.ds(parity, rows, stride=RATIO)] += change_n[f * rows : (f + 1) * rows]
        stores.append(
            pltpu.make_async_copy(fine.at[:, n], out.at[:, :, pl.ds(n * lanes, lanes)], store.at[n])
        )
        stores[-1].start()

    for copy in home[1:]:
        copy.wait_send()

    @pl.when(slot == 0)
    def _():
        home[0].wait_send()

    for copy in stores:
        copy.wait()


def propagate_at(propagate, acc, change, slot):
    for core in range(CORES):
        @pl.when(slot == core)
        def _():
            propagate(acc.at[0], change, core)


def shards(start_old, incoming):
    size = lax.axis_size("space")
    state = start_old[0]
    width = state.shape[2]
    fields, rows, nc = incoming.shape
    half = nc // 2
    count = half // size
    each = count // CORES
    forward, wide, turn, twiddle, inverse, east, north, sine, versine = tables(nc)
    mirror = np.eye(2 * rows, dtype=np.float32)
    east = np.repeat(east[:, None], nc, axis=1)
    north = np.repeat(north[None, :], 8, axis=0)
    operands = [state, incoming, mirror.astype(jnp.bfloat16), north, twiddle]
    distant = [*halves(wide), *halves(forward), *halves(turn), *halves(inverse)]
    strips = width // LANES
    padded = (fields, strips, state.shape[1] + 4 * HALO, LANES)
    blocks = (size, CORES, fields, each, 2 * rows)
    single = (size, fields, each, 2 * rows)
    whole = (fields, each, 2 * nc)
    shapes = [north.shape, twiddle.shape, (2, fields, HALO, width), padded, padded]
    shapes += [(fields, strips, state.shape[1], LANES)]
    shapes += [blocks] * 4 + [single] + [(CORES, *whole)] * 2 + [whole] * 2
    shapes += [blocks, single, blocks] + [(count, nc)] * 3
    buffers = [pltpu.VMEM(incoming.shape, jnp.float32)]
    buffers += [pltpu.VMEM(mirror.shape, jnp.bfloat16)]
    buffers += [pltpu.VMEM(shape, jnp.float32) for shape in shapes]
    far = pl.BlockSpec(memory_space=pltpu.HBM)
    inputs = len(operands) + len(distant) + 3
    dma = pltpu.SemaphoreType.DMA
    result = pl.pallas_call(
        functools.partial(kernel, size),
        out_shape=jax.ShapeDtypeStruct(state.shape, jnp.float32),
        in_specs=[far] * inputs,
        out_specs=far,
        scratch_shapes=buffers
        + [pltpu.VMEM(table.shape, jnp.bfloat16) for table in distant]
        + [dma((inputs + strips,)), dma((strips,))]
        + [dma((2,))] * 4
        + [dma((size,))] * 4
        + [dma((size, CORES)), dma((size,)), dma((size,)), dma((size, CORES))],
        compiler_params=pltpu.CompilerParams(
            collective_id=0, has_side_effects=True, vmem_limit_bytes=(64 << 20) - (128 << 10)
        ),
        cost_estimate=pl.CostEstimate(
            flops=40 * fields * count * nc * nc, bytes_accessed=32 * nc * nc, transcendentals=0
        ),
    )(*operands, *distant, east, sine, versine)
    return result[None]


def solution(mesh):
    placed = (P(("group", "tm"), None, "space", None), P("group", "space", None))
    return jax.shard_map(
        shards,
        mesh=mesh,
        in_specs=placed,
        out_specs=P(("group", "tm"), None, "space", None),
        check_vma=False,
    )
```

```python
import functools
import math

import jax
import jax.numpy as jnp
import numpy as np
from jax import lax
from jax.experimental import pallas as pl
from jax.experimental.pallas import tpu as pltpu
from jax.sharding import PartitionSpec as P

RATIO = 2
STEPS = 2
TIME_STEP = 0.25
CORIOLIS = 0.5
HALO = 8
RIM = 4
CORES = 2
LANES = 128
MESH = pl.DeviceIdType.MESH


def halves(table):
    high = table.astype(jnp.bfloat16)
    return high, (table - high.astype(np.float32)).astype(jnp.bfloat16)


def split(a):
    high = a.astype(jnp.bfloat16)
    return high, (a - high.astype(jnp.float32)).astype(jnp.bfloat16)


def dot(a, b, sides=(1, 0)):
    dims = (((sides[0],), (sides[1],)), ((), ()))
    return lax.dot_general(a, b, dims, preferred_element_type=jnp.float32)


def dot_split(a, high, low):
    up, down = split(a)
    count = a.shape[0]
    both = dot(jnp.concatenate([up, down], 0), high)
    return both[:count] + (both[count:] + dot(up, low))


def dot_table(high, low, a):
    up, down = split(a)
    count = a.shape[0]
    both = dot(high, jnp.concatenate([up, down], 0), (1, 1))
    return both[:, :count] + (both[:, count:] + dot(low, up, (1, 1)))


def tables(nc):
    half = nc // 2
    order = np.concatenate([np.arange(0, half, 2), np.arange(1, half, 2)])
    angle = 2.0 * math.pi / nc * (np.outer(order, np.arange(half)) % nc)
    real, imag = np.cos(angle), -np.sin(angle)
    imag[0] = (-1.0) ** np.arange(half)
    scale = np.full((half, 1), 2.0 / (nc * nc))
    scale[0] = 1.0 / (nc * nc)
    halved = lambda a: a.reshape(2, half // 2, half)
    forward = np.stack([halved(real), halved(imag)], 1).reshape(2, half, half)
    inverse = np.stack([halved(real * scale), halved(imag * scale)], 1).reshape(2, half, half)
    wide = np.repeat(forward / RATIO**2, RATIO, axis=2)
    inverse = np.repeat(inverse, RATIO, axis=2)

    y = np.arange(half)
    angle = 2.0 * math.pi / half * (np.outer(y, y) % half)
    turn = np.concatenate([np.cos(angle), np.sin(angle)], 1)
    angle = 2.0 * math.pi / nc * y
    twiddle = np.repeat(np.stack([np.cos(angle), -np.sin(angle)])[:, None], 8, axis=1)

    index = np.arange(nc)
    index = np.where(index < half, index, index - nc)
    index = np.where(index == -half, 0, index)
    wave = index * (2.0 * math.pi / (nc * RATIO))
    east = wave[order]
    north = np.concatenate([wave[0::2], wave[1::2]])
    omega = np.sqrt(CORIOLIS**2 + east[:, None] ** 2 + north[None, :] ** 2)
    duration = STEPS * TIME_STEP
    sine = np.sin(omega * duration) / omega
    versine = (1.0 - np.cos(omega * duration)) / omega**2
    single = lambda a: np.asarray(a, np.float32)
    return [single(a) for a in (forward, wide, turn, twiddle, inverse, east, north, sine, versine)]


def slopes(ref, at):
    blocks, lanes = ref.shape[1], ref.shape[3]
    lane = lax.broadcasted_iota(jnp.int32, (8, lanes), 1)
    begin, end = lane == 0, lane == lanes - 1
    mids = [[None] * blocks for _ in range(3)]
    rights = [[None] * blocks for _ in range(3)]
    lefts = [[None] * blocks for _ in range(3)]

    def mid(f, n):
        if mids[f][n] is None:
            mids[f][n] = ref[f, n, pl.ds(at, 8)]
        return mids[f][n]

    def right(f, n):
        if rights[f][n] is None:
            rights[f][n] = pltpu.roll(mid(f, n), 1, 1)
        return rights[f][n]

    def left(f, n):
        if lefts[f][n] is None:
            lefts[f][n] = pltpu.roll(mid(f, n), lanes - 1, 1)
        return lefts[f][n]

    for n in range(blocks):
        before, after = (n - 1) % blocks, (n + 1) % blocks
        hw, uw, vw = (jnp.where(begin, right(f, before), right(f, n)) for f in range(3))
        he, ue, ve = (jnp.where(end, left(f, after), left(f, n)) for f in range(3))
        hs, us, vs = (ref[f, n, pl.ds(at - 1, 8)] for f in range(3))
        hn, un, vn = (ref[f, n, pl.ds(at + 1, 8)] for f in range(3))
        h, u, v = (mid(f, n) for f in range(3))
        ux, vy = ue - uw, vn - vs
        rate_h = (ux + (he * ue - hw * uw)) + (vy + (hn * vn - hs * vs))
        rate_u = (u * ux + v * (un - us)) + ((he - hw) - v)
        rate_v = (u * (ve - vw) + v * vy) + ((hn - hs) + u)
        yield n, (h, u, v), (rate_h, rate_u, rate_v)


def loop(start, stop, body):
    count = stop - start
    if count > 0:
        unroll = max(n for n in range(1, 9) if count % n == 0)
        lax.fori_loop(start, stop, lambda n, _: body(n), None, unroll=unroll)


def heun(rows, now, first, fine):
    blocks = (rows + 2 * HALO) // 8
    unit = 0.5 * TIME_STEP

    def rows_at(block):
        return pl.multiple_of(block * 8, 8)

    def predict(block):
        at = rows_at(block + 1)
        found = [(f, n, mid[f] - unit * rate[f]) for n, mid, rate in slopes(now, at) for f in range(3)]
        for f, n, value in found:
            first[f, n, pl.ds(at, 8)] = value

    def correct(out, shift):
        def body(block):
            at, to = rows_at(block + 1), rows_at(block + 1 - shift)
            found = [
                (f, n, 0.5 * (now[f, n, pl.ds(at, 8)] + mid[f]) - (0.5 * unit) * rate[f])
                for n, mid, rate in slopes(first, at)
                for f in range(3)
            ]
            for f, n, value in found:
                out[f, n, pl.ds(to, 8)] = value

        return body

    stages = [(predict, 0), (correct(now, 0), 0), (predict, 0), (correct(fine, 2), 1)]

    def inside():
        for depth, (body, _) in enumerate(stages):
            loop(2 + depth, blocks - 2 - depth, body)

    def outside():
        for depth, (body, begin) in enumerate(stages):
            low, high = 2 + depth, blocks - 2 - depth
            if low < high:
                side = low - begin
                skip = high - low
                loop(0, 2 * side, lambda n: body(jnp.where(n < side, n, n + skip) + begin))
            else:
                loop(begin, blocks - begin, body)

    return inside, outside


def apply_operator(s, a, b):
    (hr, hi), (ur, ui), (vr, vi) = s
    return (
        (a * ui + b * vi, -(a * ur + b * vr)),
        (a * hi + CORIOLIS * vr, CORIOLIS * vi - a * hr),
        (b * hi - CORIOLIS * ur, -(b * hr) - CORIOLIS * ui),
    )


def kernel(
    size, state, incoming_far, mirror_far, north_far, twiddle_far,
    wide_h_far, wide_l_far, short_h_far, short_l_far, turn_h, turn_l, inverse_h, inverse_l,
    east_far, sine_far, versine_far, fine,
    incoming, mirror, north, twiddle, rim_in, now, first, gap, mine, theirs, landed, arrived, acc, kept, relayed, change,
    leaving, going, returned, east, sine, versine,
    wide_h, wide_l, short_h, short_l, th, tl, ih, il,
    fetch, rim_send, rim_recv, t_send, t_recv, d_send, d_recv, e_send, e_recv, g_send, g_recv, h_send, h_recv,
):
    fields, rows, nc = incoming_far.shape
    wide_rows, width = state.shape[1:]
    strips, lanes = now.shape[1], now.shape[3]
    half = nc // 2
    count = half // size
    each = count // CORES
    me, slot = lax.axis_index("space"), lax.axis_index("tm")
    peers = [lax.rem(me + d, size) for d in range(size)]
    origins = [lax.rem(me + size - d, size) for d in range(size)]

    share = pl.ds(pl.multiple_of(me * count, count), count)
    fetches = [
        pltpu.make_async_copy(source, target, fetch.at[n])
        for n, (source, target) in enumerate(
            (
                *(
                    (state.at[:, :, pl.ds(n * lanes, lanes)], now.at[:, n, pl.ds(2 * HALO, wide_rows)])
                    for n in range(strips)
                ),
                (wide_h_far, wide_h),
                (wide_l_far, wide_l),
                (incoming_far, incoming),
                (short_h_far, short_h),
                (short_l_far, short_l),
                (turn_h, th),
                (turn_l, tl),
                (twiddle_far, twiddle),
                (north_far, north),
                (east_far.at[share], east),
                (sine_far.at[share], sine),
                (versine_far.at[share], versine),
                (mirror_far, mirror),
                (inverse_h, ih),
                (inverse_l, il),
            )
        )
    ]
    rim_in[...] = jnp.zeros_like(rim_in)
    pad = jnp.zeros((fields, strips, HALO, lanes), jnp.float32)
    for ref in (now, first):
        ref[:, :, :HALO] = pad
        ref[:, :, 3 * HALO + wide_rows :] = pad

    barrier = pltpu.get_barrier_semaphore()
    for d, peer in enumerate(peers):
        for core in range(CORES):
            if d > 0:
                pl.semaphore_signal(barrier, inc=1, device_id={"space": peer, "tm": core}, device_id_type=MESH)
    pl.semaphore_signal(barrier, inc=1, device_id={"tm": 1 - slot}, device_id_type=MESH)
    for copy in fetches[: strips + 5]:
        copy.start()

    def send(source, target, sender, receiver, peer, core):
        return pltpu.make_async_remote_copy(
            src_ref=source, dst_ref=target, send_sem=sender, recv_sem=receiver,
            device_id={"space": peer, "tm": core}, device_id_type=MESH,
        )

    rims = [
        send(
            state.at[:, pl.ds(source, RIM)], rim_in.at[n, :, pl.ds(target, RIM)],
            rim_send.at[n], rim_recv.at[n], peer, slot,
        )
        for n, (source, target, peer) in enumerate(
            ((wide_rows - RIM, HALO - RIM, peers[1]), (0, 0, peers[-1]))
        )
    ]
    early = [send(gap.at[p], landed.at[me], d_send.at[n], d_recv.at[n], p, 1) for n, p in enumerate(peers)]
    ahead = send(gap, theirs, t_send.at[0], t_recv.at[0], me, 0)
    relay = send(kept.at[0], relayed, t_send.at[1], t_recv.at[1], me, 0)
    back = [send(leaving.at[p], returned.at[me], e_send.at[n], e_recv.at[n], p, 0) for n, p in enumerate(peers)]
    late = [
        [send(mine.at[p, c], arrived.at[me], g_send.at[n, c], g_recv.at[n], p, c) for c in range(CORES)]
        for n, p in enumerate(peers)
    ]
    home = [
        send(going.at[p], returned.at[me, slot], h_send.at[n], h_recv.at[n, slot], p, 1)
        for n, p in enumerate(peers)
    ]
    homes = [
        [send(going.at[p], returned.at[me, c], h_send.at[n], h_recv.at[n, c], p, 1) for c in range(CORES)]
        for n, p in enumerate(peers)
    ]

    def x_spectra(value, high, low, put):
        middle = value.shape[1] // 2
        west, east_side = value[:, :middle], value[:, middle:]
        for parity, part in enumerate((west + east_side, west - east_side)):
            found = dot_table(high[parity], low[parity], part)
            for f in range(fields):
                both = found[:, f * rows : (f + 1) * rows]
                both = jnp.concatenate([both[: half // 2], both[half // 2 :]], 1)
                for n in range(size * CORES // 2):
                    j, c = divmod(parity * size * CORES // 2 + n, CORES)
                    put((j, c, f), both[n * each : (n + 1) * each])

    def paired(ref, start):
        parts = [
            jnp.concatenate(
                [
                    ref[f, n, pl.ds(start, rows, stride=2)] + ref[f, n, pl.ds(start + 1, rows, stride=2)]
                    for n in range(strips)
                ],
                1,
            )
            for f in range(fields)
        ]
        return jnp.concatenate(parts, 0)

    for copy in fetches[: strips + 2]:
        copy.wait()

    def put_gap(at, value):
        gap[at] = -value

    def add_gap(at, value):
        gap[at] += value

    def put_mine(at, value):
        mine[at] = theirs[at] + value

    x_spectra(paired(now, 16), wide_h, wide_l, put_gap)
    for copy in fetches[strips + 2 : strips + 5]:
        copy.wait()

    @pl.when(slot == 0)
    def _():
        fresh = jnp.concatenate([incoming[f] for f in range(fields)], 0)
        x_spectra(fresh, short_h, short_l, add_gap)

    pl.semaphore_wait(barrier, CORES * size - 1)
    for copy in rims:
        copy.start()

    @pl.when(slot == 0)
    def _():
        for copy in early:
            copy.start()

    @pl.when(slot == 1)
    def _():
        ahead.start()

    for copy in fetches[strips + 5 :]:
        copy.start()

    inside, outside = heun(wide_rows, now, first, fine)
    inside()
    for copy in rims:
        copy.wait()
    for n in range(strips):
        across = slice(n * lanes, (n + 1) * lanes)
        now[:, n, HALO : 2 * HALO] = rim_in[0, :, :, across]
        now[:, n, 2 * HALO + wide_rows : 3 * HALO + wide_rows] = rim_in[1, :, :, across]
    outside()

    def turned(parts, sign):
        length = parts[0].shape[0]
        found = dot_split(jnp.concatenate(parts, 0), th[...], tl[...])
        cos = [found[n * length : (n + 1) * length, :half] for n in range(4)]
        sin = [found[n * length : (n + 1) * length, half:] for n in range(4)]
        return [
            (cos[n] - sign * sin[n + 1], cos[n + 1] + sign * sin[n]) for n in (0, 2)
        ]

    def y_spectra(blocks):
        low, high = blocks[: size // 2], blocks[size // 2 :]
        both = [a + b for a, b in zip(low, high)]
        apart = [a - b for a, b in zip(low, high)]
        gather = lambda pieces, at: jnp.concatenate([a[:, at * rows : (at + 1) * rows] for a in pieces], 1)
        real, imag = gather(apart, 0), gather(apart, 1)
        a, b = twiddle[0, 0:1], twiddle[1, 0:1]
        (er, ei), (our, oi) = turned(
            [gather(both, 0), gather(both, 1), real * a - imag * b, real * b + imag * a], -1.0
        )
        return jnp.concatenate([er, our, ei, oi], 1)

    def y_fields(value):
        (er, ei), (our, oi) = turned([value[:, n * half : (n + 1) * half] for n in (0, 2, 1, 3)], 1.0)
        a, b = twiddle[0, 0:1], twiddle[1, 0:1]
        our, oi = our * a + oi * b, oi * a - our * b
        blocks = []
        for real, imag in ((er + our, ei + oi), (er - our, ei - oi)):
            for n in range(size // 2):
                at = slice(n * rows, (n + 1) * rows)
                blocks.append(jnp.concatenate([real[:, at], imag[:, at]], 1))
        return blocks

    def propagate(source, target, core):
        tile = min(each, 8)
        for r in range(0, each, tile):
            at = pl.ds(core * each + r, tile)
            wave = slice(r, r + tile)
            spectra = [(source[f, wave, :nc], source[f, wave, nc:]) for f in range(fields)]
            once = apply_operator(spectra, east[at], north[:tile])
            twofold = apply_operator(once, east[at], north[:tile])
            for f in range(fields):
                for part, lanes in enumerate((slice(0, nc), slice(nc, 2 * nc))):
                    target[f, wave, lanes] = (
                        spectra[f][part] + sine[at] * once[f][part] + versine[at] * twofold[f][part]
                    )

    for copy in fetches[strips + 5 :]:
        copy.wait()

    @pl.when(slot == 1)
    def _():
        for copy in early:
            copy.wait_recv()
        order = [(c, f) for c in range(CORES) for f in range(fields)]
        value = y_spectra(
            [jnp.concatenate([landed[j, c, f] for c, f in order], 0) for j in range(size)]
        )
        for n, (c, f) in enumerate(order):
            acc[c, f] = value[n * each : (n + 1) * each]
        for c in range(CORES):
            propagate(acc.at[c], kept.at[c], c)
        relay.start()
        value = y_fields(jnp.concatenate([kept[c, f] for c, f in order], 0))
        for j in range(size):
            for n, (c, f) in enumerate(order):
                leaving[j, c, f] = value[j][n * each : (n + 1) * each]
        for copy in back:
            copy.start()

    @pl.when(slot == 0)
    def _():
        for copy in early:
            copy.wait_send()
        ahead.wait_recv()
        x_spectra(paired(fine, 0), wide_h, wide_l, put_mine)
        for n in range(size):
            for c in range(CORES):
                if n > 0 or c > 0:
                    late[n][c].start()
        arrived[me] = mine[me, 0]
        relay.wait_recv()

    @pl.when(slot == 1)
    def _():
        relay.wait_send()
        relayed[...] = kept[1]
        late[0][1].wait_recv()

    for n in range(1, size):
        late[n][0].wait_recv()
    value = y_spectra([jnp.concatenate([arrived[j, f] for f in range(fields)], 0) for j in range(size)])
    for f in range(fields):
        acc[0, f] = value[f * each : (f + 1) * each] + relayed[f]

    propagate_at(propagate, acc, change, slot)
    value = y_fields(jnp.concatenate([change[f] for f in range(fields)], 0))
    for j in range(size):
        for f in range(fields):
            going[j, f] = value[j][f * each : (f + 1) * each]
    for copy in home[1:]:
        copy.start()

    @pl.when(slot == 0)
    def _():
        home[0].start()
        for n in range(size):
            for c in range(CORES):
                if n > 0 or c > 0:
                    late[n][c].wait_send()
        for copy in back:
            copy.wait_recv()

    @pl.when(slot == 1)
    def _():
        returned[me, 1] = going[me]
        ahead.wait_send()
        for copy in back:
            copy.wait_send()
        homes[0][0].wait_recv()
        for n in range(1, size):
            for c in range(CORES):
                homes[n][c].wait_recv()

    turned_up, turned_down = [], []
    for f in range(fields):
        spectrum = jnp.concatenate([returned[j, c, f] for j in range(size) for c in range(CORES)], 0)
        for part, parts in zip(split(spectrum), (turned_up, turned_down)):
            wide_part = dot(mirror[...], part, (1, 1)).astype(jnp.bfloat16)
            parts.append([wide_part[:rows], wide_part[rows:]])
    sums = []
    for parity in range(2):
        at = slice(parity * half // 2, (parity + 1) * half // 2)
        up, down = (
            jnp.concatenate([jnp.concatenate([real[:, at], imag[:, at]], 1) for real, imag in parts], 0)
            for parts in (turned_up, turned_down)
        )
        both = dot(jnp.concatenate([up, down], 0), ih[parity])
        sums.append(both[: up.shape[0]] + (both[up.shape[0] :] + dot(up, il[parity])))
    for n in range(strips):
        at = n % (strips // 2) * lanes
        even, odd = (a[:, at : at + lanes] for a in sums)
        change_n = even + odd if n < strips // 2 else even - odd
        for f in range(fields):
            for parity in range(RATIO):
                fine[f, n, pl.ds(parity, rows, stride=RATIO)] += change_n[f * rows : (f + 1) * rows]

    for copy in home[1:]:
        copy.wait_send()

    @pl.when(slot == 0)
    def _():
        home[0].wait_send()


def hand_over(fine, out, sem):
    strips, lanes = fine.shape[1], fine.shape[3]
    copies = [
        pltpu.make_async_copy(fine.at[:, n], out.at[:, :, pl.ds(n * lanes, lanes)], sem.at[n])
        for n in range(strips)
    ]
    for copy in copies:
        copy.start()
    for copy in copies:
        copy.wait()


def propagate_at(propagate, acc, change, slot):
    for core in range(CORES):
        @pl.when(slot == core)
        def _():
            propagate(acc.at[0], change, core)


def shards(start_old, incoming):
    size = lax.axis_size("space")
    state = start_old[0]
    width = state.shape[2]
    fields, rows, nc = incoming.shape
    half = nc // 2
    count = half // size
    each = count // CORES
    forward, wide, turn, twiddle, inverse, east, north, sine, versine = tables(nc)
    mirror = np.eye(2 * rows, dtype=np.float32)
    east = np.repeat(east[:, None], nc, axis=1)
    north = np.repeat(north[None, :], 8, axis=0)
    operands = [state, incoming, mirror.astype(jnp.bfloat16), north, twiddle]
    distant = [*halves(wide), *halves(forward), *halves(turn), *halves(inverse)]
    strips = width // LANES
    padded = (fields, strips, state.shape[1] + 4 * HALO, LANES)
    blocks = (size, CORES, fields, each, 2 * rows)
    single = (size, fields, each, 2 * rows)
    whole = (fields, each, 2 * nc)
    shapes = [north.shape, twiddle.shape, (2, fields, HALO, width), padded, padded]
    shapes += [blocks] * 4 + [single] + [(CORES, *whole)] * 2 + [whole] * 2
    shapes += [blocks, single, blocks] + [(count, nc)] * 3
    buffers = [pltpu.VMEM(incoming.shape, jnp.float32)]
    buffers += [pltpu.VMEM(mirror.shape, jnp.bfloat16)]
    buffers += [pltpu.VMEM(shape, jnp.float32) for shape in shapes]
    far = pl.BlockSpec(memory_space=pltpu.HBM)
    inputs = len(operands) + len(distant) + 3
    dma = pltpu.SemaphoreType.DMA
    result = pl.pallas_call(
        functools.partial(kernel, size),
        out_shape=pltpu.VMEM((fields, strips, state.shape[1], LANES), jnp.float32),
        in_specs=[far] * inputs,
        out_specs=pl.BlockSpec(memory_space=pltpu.VMEM),
        scratch_shapes=buffers
        + [pltpu.VMEM(table.shape, jnp.bfloat16) for table in distant]
        + [dma((inputs + strips,))]
        + [dma((2,))] * 4
        + [dma((size,))] * 4
        + [dma((size, CORES)), dma((size,)), dma((size,)), dma((size, CORES))],
        compiler_params=pltpu.CompilerParams(
            collective_id=0, has_side_effects=True, vmem_limit_bytes=48 << 20
        ),
        cost_estimate=pl.CostEstimate(
            flops=40 * fields * count * nc * nc, bytes_accessed=32 * nc * nc, transcendentals=0
        ),
    )(*(pltpu.with_memory_space_constraint(a, pltpu.HBM) for a in (*operands, *distant, east, sine, versine)))
    result = pl.pallas_call(
        hand_over,
        out_shape=jax.ShapeDtypeStruct(state.shape, jnp.float32),
        in_specs=[pl.BlockSpec(memory_space=pltpu.VMEM)],
        out_specs=far,
        scratch_shapes=[dma((strips,))],
        compiler_params=pltpu.CompilerParams(vmem_limit_bytes=16 << 20),
    )(pltpu.with_memory_space_constraint(result, pltpu.VMEM))
    return result[None]


def solution(mesh):
    placed = (P(("group", "tm"), None, "space", None), P("group", "space", None))
    return jax.shard_map(
        shards,
        mesh=mesh,
        in_specs=placed,
        out_specs=P(("group", "tm"), None, "space", None),
        check_vma=False,
    )
```

```python
import functools
import math

import jax
import jax.numpy as jnp
import numpy as np
from jax import lax
from jax.experimental import pallas as pl
from jax.experimental.pallas import tpu as pltpu
from jax.sharding import PartitionSpec as P

RATIO = 2
STEPS = 2
TIME_STEP = 0.25
CORIOLIS = 0.5
HALO = 8
RIM = 4
CORES = 2
LANES = 128
MESH = pl.DeviceIdType.MESH


def halves(table):
    high = table.astype(jnp.bfloat16)
    return high, (table - high.astype(np.float32)).astype(jnp.bfloat16)


def split(a):
    high = a.astype(jnp.bfloat16)
    return high, (a - high.astype(jnp.float32)).astype(jnp.bfloat16)


def dot(a, b, sides=(1, 0)):
    dims = (((sides[0],), (sides[1],)), ((), ()))
    return lax.dot_general(a, b, dims, preferred_element_type=jnp.float32)


def dot_split(a, high, low):
    up, down = split(a)
    count = a.shape[0]
    both = dot(jnp.concatenate([up, down], 0), high)
    return both[:count] + (both[count:] + dot(up, low))


def dot_table(high, low, a):
    up, down = split(a)
    count = a.shape[0]
    both = dot(high, jnp.concatenate([up, down], 0), (1, 1))
    return both[:, :count] + (both[:, count:] + dot(low, up, (1, 1)))


def tables(nc):
    half = nc // 2
    order = np.concatenate([np.arange(0, half, 2), np.arange(1, half, 2)])
    angle = 2.0 * math.pi / nc * (np.outer(order, np.arange(half)) % nc)
    real, imag = np.cos(angle), -np.sin(angle)
    imag[0] = (-1.0) ** np.arange(half)
    scale = np.full((half, 1), 2.0 / (nc * nc))
    scale[0] = 1.0 / (nc * nc)
    halved = lambda a: a.reshape(2, half // 2, half)
    forward = np.stack([halved(real), halved(imag)], 1).reshape(2, half, half)
    inverse = np.stack([halved(real * scale), halved(imag * scale)], 1).reshape(2, half, half)
    wide = np.repeat(forward / RATIO**2, RATIO, axis=2)
    inverse = np.repeat(inverse, RATIO, axis=2)

    y = np.arange(half)
    angle = 2.0 * math.pi / half * (np.outer(y, y) % half)
    turn = np.concatenate([np.cos(angle), np.sin(angle)], 1)
    angle = 2.0 * math.pi / nc * y
    twiddle = np.repeat(np.stack([np.cos(angle), -np.sin(angle)])[:, None], 8, axis=1)

    index = np.arange(nc)
    index = np.where(index < half, index, index - nc)
    index = np.where(index == -half, 0, index)
    wave = index * (2.0 * math.pi / (nc * RATIO))
    east = wave[order]
    north = np.concatenate([wave[0::2], wave[1::2]])
    omega = np.sqrt(CORIOLIS**2 + east[:, None] ** 2 + north[None, :] ** 2)
    duration = STEPS * TIME_STEP
    sine = np.sin(omega * duration) / omega
    versine = (1.0 - np.cos(omega * duration)) / omega**2
    single = lambda a: np.asarray(a, np.float32)
    return [single(a) for a in (forward, wide, turn, twiddle, inverse, east, north, sine, versine)]


def slopes(ref, at):
    blocks, lanes = ref.shape[1], ref.shape[3]
    lane = lax.broadcasted_iota(jnp.int32, (8, lanes), 1)
    begin, end = lane == 0, lane == lanes - 1
    mids = [[None] * blocks for _ in range(3)]
    rights = [[None] * blocks for _ in range(3)]
    lefts = [[None] * blocks for _ in range(3)]

    def mid(f, n):
        if mids[f][n] is None:
            mids[f][n] = ref[f, n, pl.ds(at, 8)]
        return mids[f][n]

    def right(f, n):
        if rights[f][n] is None:
            rights[f][n] = pltpu.roll(mid(f, n), 1, 1)
        return rights[f][n]

    def left(f, n):
        if lefts[f][n] is None:
            lefts[f][n] = pltpu.roll(mid(f, n), lanes - 1, 1)
        return lefts[f][n]

    for n in range(blocks):
        before, after = (n - 1) % blocks, (n + 1) % blocks
        hw, uw, vw = (jnp.where(begin, right(f, before), right(f, n)) for f in range(3))
        he, ue, ve = (jnp.where(end, left(f, after), left(f, n)) for f in range(3))
        hs, us, vs = (ref[f, n, pl.ds(at - 1, 8)] for f in range(3))
        hn, un, vn = (ref[f, n, pl.ds(at + 1, 8)] for f in range(3))
        h, u, v = (mid(f, n) for f in range(3))
        ux, vy = ue - uw, vn - vs
        rate_h = (ux + (he * ue - hw * uw)) + (vy + (hn * vn - hs * vs))
        rate_u = (u * ux + v * (un - us)) + ((he - hw) - v)
        rate_v = (u * (ve - vw) + v * vy) + ((hn - hs) + u)
        yield n, (h, u, v), (rate_h, rate_u, rate_v)


def loop(start, stop, body):
    count = stop - start
    if count > 0:
        unroll = max(n for n in range(1, 9) if count % n == 0)
        lax.fori_loop(start, stop, lambda n, _: body(n), None, unroll=unroll)


def heun(rows, now, first, fine):
    blocks = (rows + 2 * HALO) // 8
    unit = 0.5 * TIME_STEP

    def rows_at(block):
        return pl.multiple_of(block * 8, 8)

    def predict(block):
        at = rows_at(block + 1)
        found = [(f, n, mid[f] - unit * rate[f]) for n, mid, rate in slopes(now, at) for f in range(3)]
        for f, n, value in found:
            first[f, n, pl.ds(at, 8)] = value

    def correct(out, shift):
        def body(block):
            at, to = rows_at(block + 1), rows_at(block + 1 - shift)
            found = [
                (f, n, 0.5 * (now[f, n, pl.ds(at, 8)] + mid[f]) - (0.5 * unit) * rate[f])
                for n, mid, rate in slopes(first, at)
                for f in range(3)
            ]
            for f, n, value in found:
                out[f, n, pl.ds(to, 8)] = value

        return body

    stages = [(predict, 0), (correct(now, 0), 0), (predict, 0), (correct(fine, 2), 1)]

    def inside():
        for depth, (body, _) in enumerate(stages):
            loop(2 + depth, blocks - 2 - depth, body)

    def outside():
        for depth, (body, begin) in enumerate(stages):
            low, high = 2 + depth, blocks - 2 - depth
            if low < high:
                side = low - begin
                skip = high - low
                loop(0, 2 * side, lambda n: body(jnp.where(n < side, n, n + skip) + begin))
            else:
                loop(begin, blocks - begin, body)

    return inside, outside


def apply_operator(s, a, b):
    (hr, hi), (ur, ui), (vr, vi) = s
    return (
        (a * ui + b * vi, -(a * ur + b * vr)),
        (a * hi + CORIOLIS * vr, CORIOLIS * vi - a * hr),
        (b * hi - CORIOLIS * ur, -(b * hr) - CORIOLIS * ui),
    )


def kernel(
    size, state, incoming_far, mirror_far, north_far, twiddle_far,
    wide_h_far, wide_l_far, short_h_far, short_l_far, turn_h, turn_l, inverse_h, inverse_l,
    east_far, sine_far, versine_far, fine,
    incoming, mirror, north, twiddle, rim_in, now, first, gap, mine, theirs, landed, arrived, acc, kept, relayed, change,
    leaving, going, returned, east, sine, versine,
    wide_h, wide_l, short_h, short_l, th, tl, ih, il,
    fetch, rim_send, rim_recv, t_send, t_recv, d_send, d_recv, e_send, e_recv, g_send, g_recv, h_send, h_recv,
):
    fields, rows, nc = incoming_far.shape
    wide_rows, width = state.shape[1:]
    strips, lanes = now.shape[1], now.shape[3]
    half = nc // 2
    count = half // size
    each = count // CORES
    me, slot = lax.axis_index("space"), lax.axis_index("tm")
    peers = [lax.rem(me + d, size) for d in range(size)]
    origins = [lax.rem(me + size - d, size) for d in range(size)]

    share = pl.ds(pl.multiple_of(me * count, count), count)
    fetches = [
        pltpu.make_async_copy(source, target, fetch.at[n])
        for n, (source, target) in enumerate(
            (
                *(
                    (state.at[:, :, pl.ds(n * lanes, lanes)], now.at[:, n, pl.ds(2 * HALO, wide_rows)])
                    for n in range(strips)
                ),
                (wide_h_far, wide_h),
                (wide_l_far, wide_l),
                (incoming_far, incoming),
                (short_h_far, short_h),
                (short_l_far, short_l),
                (turn_h, th),
                (turn_l, tl),
                (twiddle_far, twiddle),
                (north_far, north),
                (east_far.at[share], east),
                (sine_far.at[share], sine),
                (versine_far.at[share], versine),
                (mirror_far, mirror),
                (inverse_h, ih),
                (inverse_l, il),
            )
        )
    ]
    rim_in[...] = jnp.zeros_like(rim_in)
    pad = jnp.zeros((fields, strips, HALO, lanes), jnp.float32)
    for ref in (now, first):
        ref[:, :, :HALO] = pad
        ref[:, :, 3 * HALO + wide_rows :] = pad

    barrier = pltpu.get_barrier_semaphore()
    for d, peer in enumerate(peers):
        for core in range(CORES):
            if d > 0:
                pl.semaphore_signal(barrier, inc=1, device_id={"space": peer, "tm": core}, device_id_type=MESH)
    pl.semaphore_signal(barrier, inc=1, device_id={"tm": 1 - slot}, device_id_type=MESH)
    for copy in fetches[: strips + 5]:
        copy.start()

    def send(source, target, sender, receiver, peer, core):
        return pltpu.make_async_remote_copy(
            src_ref=source, dst_ref=target, send_sem=sender, recv_sem=receiver,
            device_id={"space": peer, "tm": core}, device_id_type=MESH,
        )

    rims = [
        send(
            state.at[:, pl.ds(source, RIM)], rim_in.at[n, :, pl.ds(target, RIM)],
            rim_send.at[n], rim_recv.at[n], peer, slot,
        )
        for n, (source, target, peer) in enumerate(
            ((wide_rows - RIM, HALO - RIM, peers[1]), (0, 0, peers[-1]))
        )
    ]
    early = [send(gap.at[p], landed.at[me], d_send.at[n], d_recv.at[n], p, 1) for n, p in enumerate(peers)]
    ahead = send(gap, theirs, t_send.at[0], t_recv.at[0], me, 0)
    relay = send(kept.at[0], relayed, t_send.at[1], t_recv.at[1], me, 0)
    back = [send(leaving.at[p], returned.at[me], e_send.at[n], e_recv.at[n], p, 0) for n, p in enumerate(peers)]
    late = [
        [send(mine.at[p, c], arrived.at[me], g_send.at[n, c], g_recv.at[n], p, c) for c in range(CORES)]
        for n, p in enumerate(peers)
    ]
    home = [
        send(going.at[p], returned.at[me, slot], h_send.at[n], h_recv.at[n, slot], p, 1)
        for n, p in enumerate(peers)
    ]
    homes = [
        [send(going.at[p], returned.at[me, c], h_send.at[n], h_recv.at[n, c], p, 1) for c in range(CORES)]
        for n, p in enumerate(peers)
    ]

    def x_spectra(value, high, low, put):
        middle = value.shape[1] // 2
        west, east_side = value[:, :middle], value[:, middle:]
        for parity, part in enumerate((west + east_side, west - east_side)):
            found = dot_table(high[parity], low[parity], part)
            for f in range(fields):
                both = found[:, f * rows : (f + 1) * rows]
                both = jnp.concatenate([both[: half // 2], both[half // 2 :]], 1)
                for n in range(size * CORES // 2):
                    j, c = divmod(parity * size * CORES // 2 + n, CORES)
                    put((j, c, f), both[n * each : (n + 1) * each])

    def paired(ref, start):
        parts = [
            jnp.concatenate(
                [
                    ref[f, n, pl.ds(start, rows, stride=2)] + ref[f, n, pl.ds(start + 1, rows, stride=2)]
                    for n in range(strips)
                ],
                1,
            )
            for f in range(fields)
        ]
        return jnp.concatenate(parts, 0)

    for copy in fetches[: strips + 2]:
        copy.wait()

    def put_gap(at, value):
        gap[at] = -value

    def add_gap(at, value):
        gap[at] += value

    def put_mine(at, value):
        mine[at] = theirs[at] + value

    x_spectra(paired(now, 16), wide_h, wide_l, put_gap)
    pl.semaphore_wait(barrier, CORES * size - 1)
    for copy in rims:
        copy.start()

    for copy in fetches[strips + 2 : strips + 5]:
        copy.wait()

    @pl.when(slot == 0)
    def _():
        fresh = jnp.concatenate([incoming[f] for f in range(fields)], 0)
        x_spectra(fresh, short_h, short_l, add_gap)
        for copy in early:
            copy.start()

    @pl.when(slot == 1)
    def _():
        ahead.start()

    for copy in fetches[strips + 5 :]:
        copy.start()

    inside, outside = heun(wide_rows, now, first, fine)
    inside()
    for copy in rims:
        copy.wait()
    for n in range(strips):
        across = slice(n * lanes, (n + 1) * lanes)
        now[:, n, HALO : 2 * HALO] = rim_in[0, :, :, across]
        now[:, n, 2 * HALO + wide_rows : 3 * HALO + wide_rows] = rim_in[1, :, :, across]
    outside()

    def turned(parts, sign):
        length = parts[0].shape[0]
        found = dot_split(jnp.concatenate(parts, 0), th[...], tl[...])
        cos = [found[n * length : (n + 1) * length, :half] for n in range(4)]
        sin = [found[n * length : (n + 1) * length, half:] for n in range(4)]
        return [
            (cos[n] - sign * sin[n + 1], cos[n + 1] + sign * sin[n]) for n in (0, 2)
        ]

    def y_spectra(blocks):
        low, high = blocks[: size // 2], blocks[size // 2 :]
        both = [a + b for a, b in zip(low, high)]
        apart = [a - b for a, b in zip(low, high)]
        gather = lambda pieces, at: jnp.concatenate([a[:, at * rows : (at + 1) * rows] for a in pieces], 1)
        real, imag = gather(apart, 0), gather(apart, 1)
        a, b = twiddle[0, 0:1], twiddle[1, 0:1]
        (er, ei), (our, oi) = turned(
            [gather(both, 0), gather(both, 1), real * a - imag * b, real * b + imag * a], -1.0
        )
        return jnp.concatenate([er, our, ei, oi], 1)

    def y_fields(value):
        (er, ei), (our, oi) = turned([value[:, n * half : (n + 1) * half] for n in (0, 2, 1, 3)], 1.0)
        a, b = twiddle[0, 0:1], twiddle[1, 0:1]
        our, oi = our * a + oi * b, oi * a - our * b
        blocks = []
        for real, imag in ((er + our, ei + oi), (er - our, ei - oi)):
            for n in range(size // 2):
                at = slice(n * rows, (n + 1) * rows)
                blocks.append(jnp.concatenate([real[:, at], imag[:, at]], 1))
        return blocks

    def propagate(source, target, core):
        tile = min(each, 8)
        for r in range(0, each, tile):
            at = pl.ds(core * each + r, tile)
            wave = slice(r, r + tile)
            spectra = [(source[f, wave, :nc], source[f, wave, nc:]) for f in range(fields)]
            once = apply_operator(spectra, east[at], north[:tile])
            twofold = apply_operator(once, east[at], north[:tile])
            for f in range(fields):
                for part, lanes in enumerate((slice(0, nc), slice(nc, 2 * nc))):
                    target[f, wave, lanes] = (
                        spectra[f][part] + sine[at] * once[f][part] + versine[at] * twofold[f][part]
                    )

    for copy in fetches[strips + 5 :]:
        copy.wait()

    @pl.when(slot == 1)
    def _():
        for copy in early:
            copy.wait_recv()
        order = [(c, f) for c in range(CORES) for f in range(fields)]
        value = y_spectra(
            [jnp.concatenate([landed[j, c, f] for c, f in order], 0) for j in range(size)]
        )
        for n, (c, f) in enumerate(order):
            acc[c, f] = value[n * each : (n + 1) * each]
        for c in range(CORES):
            propagate(acc.at[c], kept.at[c], c)
        relay.start()
        value = y_fields(jnp.concatenate([kept[c, f] for c, f in order], 0))
        for j in range(size):
            for n, (c, f) in enumerate(order):
                leaving[j, c, f] = value[j][n * each : (n + 1) * each]
        for copy in back:
            copy.start()

    @pl.when(slot == 0)
    def _():
        ahead.wait_recv()
        x_spectra(paired(fine, 0), wide_h, wide_l, put_mine)
        for n in range(size):
            for c in range(CORES):
                if n > 0 or c > 0:
                    late[n][c].start()
        arrived[me] = mine[me, 0]
        relay.wait_recv()

    @pl.when(slot == 1)
    def _():
        relay.wait_send()
        relayed[...] = kept[1]
        late[0][1].wait_recv()

    for n in range(1, size):
        late[n][0].wait_recv()
    value = y_spectra([jnp.concatenate([arrived[j, f] for f in range(fields)], 0) for j in range(size)])
    for f in range(fields):
        acc[0, f] = value[f * each : (f + 1) * each] + relayed[f]

    propagate_at(propagate, acc, change, slot)
    value = y_fields(jnp.concatenate([change[f] for f in range(fields)], 0))
    for j in range(size):
        for f in range(fields):
            going[j, f] = value[j][f * each : (f + 1) * each]
    for copy in home[1:]:
        copy.start()

    @pl.when(slot == 0)
    def _():
        home[0].start()
        for n in range(size):
            for c in range(CORES):
                if n > 0 or c > 0:
                    late[n][c].wait_send()
        for copy in early:
            copy.wait_send()
        for copy in back:
            copy.wait_recv()

    @pl.when(slot == 1)
    def _():
        returned[me, 1] = going[me]
        ahead.wait_send()
        for copy in back:
            copy.wait_send()
        homes[0][0].wait_recv()
        for n in range(1, size):
            for c in range(CORES):
                homes[n][c].wait_recv()

    turned_up, turned_down = [], []
    for f in range(fields):
        spectrum = jnp.concatenate([returned[j, c, f] for j in range(size) for c in range(CORES)], 0)
        for part, parts in zip(split(spectrum), (turned_up, turned_down)):
            wide_part = dot(mirror[...], part, (1, 1)).astype(jnp.bfloat16)
            parts.append([wide_part[:rows], wide_part[rows:]])
    sums = []
    for parity in range(2):
        at = slice(parity * half // 2, (parity + 1) * half // 2)
        up, down = (
            jnp.concatenate([jnp.concatenate([real[:, at], imag[:, at]], 1) for real, imag in parts], 0)
            for parts in (turned_up, turned_down)
        )
        both = dot(jnp.concatenate([up, down], 0), ih[parity])
        sums.append(both[: up.shape[0]] + (both[up.shape[0] :] + dot(up, il[parity])))
    for n in range(strips):
        at = n % (strips // 2) * lanes
        even, odd = (a[:, at : at + lanes] for a in sums)
        change_n = even + odd if n < strips // 2 else even - odd
        for f in range(fields):
            for parity in range(RATIO):
                fine[f, n, pl.ds(parity, rows, stride=RATIO)] += change_n[f * rows : (f + 1) * rows]

    for copy in home[1:]:
        copy.wait_send()

    @pl.when(slot == 0)
    def _():
        home[0].wait_send()


def hand_over(fine, out, sem):
    strips, lanes = fine.shape[1], fine.shape[3]
    copies = [
        pltpu.make_async_copy(fine.at[:, n], out.at[:, :, pl.ds(n * lanes, lanes)], sem.at[n])
        for n in range(strips)
    ]
    for copy in copies:
        copy.start()
    for copy in copies:
        copy.wait()


def propagate_at(propagate, acc, change, slot):
    for core in range(CORES):
        @pl.when(slot == core)
        def _():
            propagate(acc.at[0], change, core)


def shards(start_old, incoming):
    size = lax.axis_size("space")
    state = start_old[0]
    width = state.shape[2]
    fields, rows, nc = incoming.shape
    half = nc // 2
    count = half // size
    each = count // CORES
    forward, wide, turn, twiddle, inverse, east, north, sine, versine = tables(nc)
    mirror = np.eye(2 * rows, dtype=np.float32)
    east = np.repeat(east[:, None], nc, axis=1)
    north = np.repeat(north[None, :], 8, axis=0)
    operands = [state, incoming, mirror.astype(jnp.bfloat16), north, twiddle]
    distant = [*halves(wide), *halves(forward), *halves(turn), *halves(inverse)]
    strips = width // LANES
    padded = (fields, strips, state.shape[1] + 4 * HALO, LANES)
    blocks = (size, CORES, fields, each, 2 * rows)
    single = (size, fields, each, 2 * rows)
    whole = (fields, each, 2 * nc)
    shapes = [north.shape, twiddle.shape, (2, fields, HALO, width), padded, padded]
    shapes += [blocks] * 4 + [single] + [(CORES, *whole)] * 2 + [whole] * 2
    shapes += [blocks, single, blocks] + [(count, nc)] * 3
    buffers = [pltpu.VMEM(incoming.shape, jnp.float32)]
    buffers += [pltpu.VMEM(mirror.shape, jnp.bfloat16)]
    buffers += [pltpu.VMEM(shape, jnp.float32) for shape in shapes]
    far = pl.BlockSpec(memory_space=pltpu.HBM)
    inputs = len(operands) + len(distant) + 3
    dma = pltpu.SemaphoreType.DMA
    result = pl.pallas_call(
        functools.partial(kernel, size),
        out_shape=pltpu.VMEM((fields, strips, state.shape[1], LANES), jnp.float32),
        in_specs=[far] * inputs,
        out_specs=pl.BlockSpec(memory_space=pltpu.VMEM),
        scratch_shapes=buffers
        + [pltpu.VMEM(table.shape, jnp.bfloat16) for table in distant]
        + [dma((inputs + strips,))]
        + [dma((2,))] * 4
        + [dma((size,))] * 4
        + [dma((size, CORES)), dma((size,)), dma((size,)), dma((size, CORES))],
        compiler_params=pltpu.CompilerParams(
            collective_id=0, has_side_effects=True, vmem_limit_bytes=48 << 20
        ),
        cost_estimate=pl.CostEstimate(
            flops=40 * fields * count * nc * nc, bytes_accessed=32 * nc * nc, transcendentals=0
        ),
    )(*(pltpu.with_memory_space_constraint(a, pltpu.HBM) for a in (*operands, *distant, east, sine, versine)))
    result = pl.pallas_call(
        hand_over,
        out_shape=jax.ShapeDtypeStruct(state.shape, jnp.float32),
        in_specs=[pl.BlockSpec(memory_space=pltpu.VMEM)],
        out_specs=far,
        scratch_shapes=[dma((strips,))],
        compiler_params=pltpu.CompilerParams(vmem_limit_bytes=16 << 20),
    )(pltpu.with_memory_space_constraint(result, pltpu.VMEM))
    return result[None]


def solution(mesh):
    placed = (P(("group", "tm"), None, "space", None), P("group", "space", None))
    return jax.shard_map(
        shards,
        mesh=mesh,
        in_specs=placed,
        out_specs=P(("group", "tm"), None, "space", None),
        check_vma=False,
    )
```

```python
import functools
import math

import jax
import jax.numpy as jnp
import numpy as np
from jax import lax
from jax.experimental import pallas as pl
from jax.experimental.pallas import tpu as pltpu
from jax.sharding import PartitionSpec as P

RATIO = 2
STEPS = 2
TIME_STEP = 0.25
CORIOLIS = 0.5
HALO = 8
RIM = 4
CORES = 2
LANES = 128
MESH = pl.DeviceIdType.MESH


def halves(table):
    high = table.astype(jnp.bfloat16)
    return high, (table - high.astype(np.float32)).astype(jnp.bfloat16)


def split(a):
    high = a.astype(jnp.bfloat16)
    return high, (a - high.astype(jnp.float32)).astype(jnp.bfloat16)


def dot(a, b, sides=(1, 0)):
    dims = (((sides[0],), (sides[1],)), ((), ()))
    return lax.dot_general(a, b, dims, preferred_element_type=jnp.float32)


def dot_split(a, high, low):
    up, down = split(a)
    count = a.shape[0]
    both = dot(jnp.concatenate([up, down], 0), high)
    return both[:count] + (both[count:] + dot(up, low))


def dot_table(high, low, a):
    up, down = split(a)
    count = a.shape[0]
    both = dot(high, jnp.concatenate([up, down], 0), (1, 1))
    return both[:, :count] + (both[:, count:] + dot(low, up, (1, 1)))


def tables(nc):
    half = nc // 2
    order = np.concatenate([np.arange(0, half, 2), np.arange(1, half, 2)])
    angle = 2.0 * math.pi / nc * (np.outer(order, np.arange(half)) % nc)
    real, imag = np.cos(angle), -np.sin(angle)
    imag[0] = (-1.0) ** np.arange(half)
    scale = np.full((half, 1), 2.0 / (nc * nc))
    scale[0] = 1.0 / (nc * nc)
    halved = lambda a: a.reshape(2, half // 2, half)
    forward = np.stack([halved(real), halved(imag)], 1).reshape(2, half, half)
    inverse = np.stack([halved(real * scale), halved(imag * scale)], 1).reshape(2, half, half)
    wide = np.repeat(forward / RATIO**2, RATIO, axis=2)
    inverse = np.repeat(inverse, RATIO, axis=2)

    y = np.arange(half)
    angle = 2.0 * math.pi / half * (np.outer(y, y) % half)
    turn = np.concatenate([np.cos(angle), np.sin(angle)], 1)
    angle = 2.0 * math.pi / nc * y
    twiddle = np.repeat(np.stack([np.cos(angle), -np.sin(angle)])[:, None], 8, axis=1)

    index = np.arange(nc)
    index = np.where(index < half, index, index - nc)
    index = np.where(index == -half, 0, index)
    wave = index * (2.0 * math.pi / (nc * RATIO))
    east = wave[order]
    north = np.concatenate([wave[0::2], wave[1::2]])
    omega = np.sqrt(CORIOLIS**2 + east[:, None] ** 2 + north[None, :] ** 2)
    duration = STEPS * TIME_STEP
    sine = np.sin(omega * duration) / omega
    versine = (1.0 - np.cos(omega * duration)) / omega**2
    single = lambda a: np.asarray(a, np.float32)
    return [single(a) for a in (forward, wide, turn, twiddle, inverse, east, north, sine, versine)]


def slopes(ref, at):
    blocks, lanes = ref.shape[1], ref.shape[3]
    lane = lax.broadcasted_iota(jnp.int32, (8, lanes), 1)
    begin, end = lane == 0, lane == lanes - 1
    mids = [[None] * blocks for _ in range(3)]
    rights = [[None] * blocks for _ in range(3)]
    lefts = [[None] * blocks for _ in range(3)]

    def mid(f, n):
        if mids[f][n] is None:
            mids[f][n] = ref[f, n, pl.ds(at, 8)]
        return mids[f][n]

    def right(f, n):
        if rights[f][n] is None:
            rights[f][n] = pltpu.roll(mid(f, n), 1, 1)
        return rights[f][n]

    def left(f, n):
        if lefts[f][n] is None:
            lefts[f][n] = pltpu.roll(mid(f, n), lanes - 1, 1)
        return lefts[f][n]

    for n in range(blocks):
        before, after = (n - 1) % blocks, (n + 1) % blocks
        hw, uw, vw = (jnp.where(begin, right(f, before), right(f, n)) for f in range(3))
        he, ue, ve = (jnp.where(end, left(f, after), left(f, n)) for f in range(3))
        hs, us, vs = (ref[f, n, pl.ds(at - 1, 8)] for f in range(3))
        hn, un, vn = (ref[f, n, pl.ds(at + 1, 8)] for f in range(3))
        h, u, v = (mid(f, n) for f in range(3))
        ux, vy = ue - uw, vn - vs
        rate_h = (ux + (he * ue - hw * uw)) + (vy + (hn * vn - hs * vs))
        rate_u = (u * ux + v * (un - us)) + ((he - hw) - v)
        rate_v = (u * (ve - vw) + v * vy) + ((hn - hs) + u)
        yield n, (h, u, v), (rate_h, rate_u, rate_v)


def loop(start, stop, body):
    count = stop - start
    if count > 0:
        unroll = max(n for n in range(1, 9) if count % n == 0)
        lax.fori_loop(start, stop, lambda n, _: body(n), None, unroll=unroll)


def heun(rows, now, first, fine):
    blocks = (rows + 2 * HALO) // 8
    unit = 0.5 * TIME_STEP

    def rows_at(block):
        return pl.multiple_of(block * 8, 8)

    def predict(block):
        at = rows_at(block + 1)
        found = [(f, n, mid[f] - unit * rate[f]) for n, mid, rate in slopes(now, at) for f in range(3)]
        for f, n, value in found:
            first[f, n, pl.ds(at, 8)] = value

    def correct(out, shift):
        def body(block):
            at, to = rows_at(block + 1), rows_at(block + 1 - shift)
            found = [
                (f, n, 0.5 * (now[f, n, pl.ds(at, 8)] + mid[f]) - (0.5 * unit) * rate[f])
                for n, mid, rate in slopes(first, at)
                for f in range(3)
            ]
            for f, n, value in found:
                out[f, n, pl.ds(to, 8)] = value

        return body

    stages = [(predict, 0), (correct(now, 0), 0), (predict, 0), (correct(fine, 2), 1)]

    def inside():
        for depth, (body, _) in enumerate(stages):
            loop(2 + depth, blocks - 2 - depth, body)

    def outside():
        for depth, (body, begin) in enumerate(stages):
            low, high = 2 + depth, blocks - 2 - depth
            if low < high:
                side = low - begin
                skip = high - low
                loop(0, 2 * side, lambda n: body(jnp.where(n < side, n, n + skip) + begin))
            else:
                loop(begin, blocks - begin, body)

    return inside, outside


def apply_operator(s, a, b):
    (hr, hi), (ur, ui), (vr, vi) = s
    return (
        (a * ui + b * vi, -(a * ur + b * vr)),
        (a * hi + CORIOLIS * vr, CORIOLIS * vi - a * hr),
        (b * hi - CORIOLIS * ur, -(b * hr) - CORIOLIS * ui),
    )


def kernel(
    size, state, incoming_far, mirror_far, north_far, twiddle_far,
    wide_h_far, wide_l_far, short_h_far, short_l_far, turn_h, turn_l, inverse_h, inverse_l,
    east_far, sine_far, versine_far, fine, sums,
    incoming, mirror, north, twiddle, rim_in, now, first, gap, mine, theirs, landed, arrived, acc, kept, change,
    leaving, going, returned, east, sine, versine,
    wide_h, wide_l, short_h, short_l, th, tl, ih, il,
    fetch, rim_send, rim_recv, t_send, t_recv, d_send, d_recv, e_send, e_recv, g_send, g_recv, h_send, h_recv,
):
    fields, rows, nc = incoming_far.shape
    wide_rows, width = state.shape[1:]
    strips, lanes = now.shape[1], now.shape[3]
    half = nc // 2
    count = half // size
    each = count // 2
    me, slot = lax.axis_index("space"), lax.axis_index("tm")
    peers = [lax.rem(me + d, size) for d in range(size)]
    origins = [lax.rem(me + size - d, size) for d in range(size)]

    share = pl.ds(pl.multiple_of(me * count, count), count)
    fetches = [
        pltpu.make_async_copy(source, target, fetch.at[n])
        for n, (source, target) in enumerate(
            (
                *(
                    (state.at[:, :, pl.ds(n * lanes, lanes)], now.at[:, n, pl.ds(2 * HALO, wide_rows)])
                    for n in range(strips)
                ),
                (wide_h_far, wide_h),
                (wide_l_far, wide_l),
                (incoming_far, incoming),
                (short_h_far, short_h),
                (short_l_far, short_l),
                (turn_h, th),
                (turn_l, tl),
                (twiddle_far, twiddle),
                (north_far, north),
                (east_far.at[share], east),
                (sine_far.at[share], sine),
                (versine_far.at[share], versine),
                (mirror_far, mirror),
                (inverse_h, ih),
                (inverse_l, il),
            )
        )
    ]
    rim_in[...] = jnp.zeros_like(rim_in)
    pad = jnp.zeros((fields, strips, HALO, lanes), jnp.float32)
    for ref in (now, first):
        ref[:, :, :HALO] = pad
        ref[:, :, 3 * HALO + wide_rows :] = pad

    barrier = pltpu.get_barrier_semaphore()
    for d, peer in enumerate(peers):
        for core in range(CORES):
            if d > 0:
                pl.semaphore_signal(barrier, inc=1, device_id={"space": peer, "tm": core}, device_id_type=MESH)
    pl.semaphore_signal(barrier, inc=1, device_id={"tm": 1 - slot}, device_id_type=MESH)
    for copy in fetches[: strips + 5]:
        copy.start()

    def send(source, target, sender, receiver, peer, core):
        return pltpu.make_async_remote_copy(
            src_ref=source, dst_ref=target, send_sem=sender, recv_sem=receiver,
            device_id={"space": peer, "tm": core}, device_id_type=MESH,
        )

    rims = [
        send(
            state.at[:, pl.ds(source, RIM)], rim_in.at[n, :, pl.ds(target, RIM)],
            rim_send.at[n], rim_recv.at[n], peer, slot,
        )
        for n, (source, target, peer) in enumerate(
            ((wide_rows - RIM, HALO - RIM, peers[1]), (0, 0, peers[-1]))
        )
    ]
    early = [send(gap.at[p], landed.at[me], d_send.at[n], d_recv.at[n], p, 1) for n, p in enumerate(peers)]
    ahead = send(gap, theirs, t_send.at[0], t_recv.at[0], me, 0)
    back = [send(leaving.at[p], returned.at[me], e_send.at[n], e_recv.at[n], p, 0) for n, p in enumerate(peers)]
    late = [
        [send(mine.at[p, h], arrived.at[me, h], g_send.at[n, h], g_recv.at[n, h], p, 1) for h in range(2)]
        for n, p in enumerate(peers)
    ]
    home = [
        [send(going.at[p, h], returned.at[me, h], h_send.at[n, h], h_recv.at[n, h], p, 1) for h in range(2)]
        for n, p in enumerate(peers)
    ]

    def x_spectra(value, high, low, put, done=None):
        middle = value.shape[1] // 2
        west, east_side = value[:, :middle], value[:, middle:]
        for parity, part in enumerate((west + east_side, west - east_side)):
            found = dot_table(high[parity], low[parity], part)
            for f in range(fields):
                both = found[:, f * rows : (f + 1) * rows]
                both = jnp.concatenate([both[: half // 2], both[half // 2 :]], 1)
                for n in range(size):
                    put((n, parity, f), both[n * each : (n + 1) * each])
            if done is not None:
                done(parity)

    def paired(ref, start):
        parts = [
            jnp.concatenate(
                [
                    ref[f, n, pl.ds(start, rows, stride=2)] + ref[f, n, pl.ds(start + 1, rows, stride=2)]
                    for n in range(strips)
                ],
                1,
            )
            for f in range(fields)
        ]
        return jnp.concatenate(parts, 0)

    for copy in fetches[: strips + 2]:
        copy.wait()

    def put_gap(at, value):
        gap[at] = -value

    def add_gap(at, value):
        gap[at] += value

    def put_mine(at, value):
        mine[at] = theirs[at] + value

    x_spectra(paired(now, 16), wide_h, wide_l, put_gap)
    pl.semaphore_wait(barrier, CORES * size - 1)
    for copy in rims:
        copy.start()

    for copy in fetches[strips + 2 : strips + 5]:
        copy.wait()

    @pl.when(slot == 0)
    def _():
        fresh = jnp.concatenate([incoming[f] for f in range(fields)], 0)
        x_spectra(fresh, short_h, short_l, add_gap)
        for copy in early:
            copy.start()

    @pl.when(slot == 1)
    def _():
        ahead.start()

    for copy in fetches[strips + 5 :]:
        copy.start()

    inside, outside = heun(wide_rows, now, first, fine)
    inside()
    for copy in rims:
        copy.wait()
    for n in range(strips):
        across = slice(n * lanes, (n + 1) * lanes)
        now[:, n, HALO : 2 * HALO] = rim_in[0, :, :, across]
        now[:, n, 2 * HALO + wide_rows : 3 * HALO + wide_rows] = rim_in[1, :, :, across]
    outside()

    def turned(parts, sign):
        length = parts[0].shape[0]
        found = dot_split(jnp.concatenate(parts, 0), th[...], tl[...])
        cos = [found[n * length : (n + 1) * length, :half] for n in range(4)]
        sin = [found[n * length : (n + 1) * length, half:] for n in range(4)]
        return [
            (cos[n] - sign * sin[n + 1], cos[n + 1] + sign * sin[n]) for n in (0, 2)
        ]

    def y_spectra(blocks):
        low, high = blocks[: size // 2], blocks[size // 2 :]
        both = [a + b for a, b in zip(low, high)]
        apart = [a - b for a, b in zip(low, high)]
        gather = lambda pieces, at: jnp.concatenate([a[:, at * rows : (at + 1) * rows] for a in pieces], 1)
        real, imag = gather(apart, 0), gather(apart, 1)
        a, b = twiddle[0, 0:1], twiddle[1, 0:1]
        (er, ei), (our, oi) = turned(
            [gather(both, 0), gather(both, 1), real * a - imag * b, real * b + imag * a], -1.0
        )
        return jnp.concatenate([er, our, ei, oi], 1)

    def y_fields(value):
        (er, ei), (our, oi) = turned([value[:, n * half : (n + 1) * half] for n in (0, 2, 1, 3)], 1.0)
        a, b = twiddle[0, 0:1], twiddle[1, 0:1]
        our, oi = our * a + oi * b, oi * a - our * b
        blocks = []
        for real, imag in ((er + our, ei + oi), (er - our, ei - oi)):
            for n in range(size // 2):
                at = slice(n * rows, (n + 1) * rows)
                blocks.append(jnp.concatenate([real[:, at], imag[:, at]], 1))
        return blocks

    def propagate(source, target, parity):
        tile = min(each, 8)
        for r in range(0, each, tile):
            at = pl.ds(parity * each + r, tile)
            wave = slice(r, r + tile)
            spectra = [(source[f, wave, :nc], source[f, wave, nc:]) for f in range(fields)]
            once = apply_operator(spectra, east[at], north[:tile])
            twofold = apply_operator(once, east[at], north[:tile])
            for f in range(fields):
                for part, lanes in enumerate((slice(0, nc), slice(nc, 2 * nc))):
                    target[f, wave, lanes] = (
                        spectra[f][part] + sine[at] * once[f][part] + versine[at] * twofold[f][part]
                    )

    for copy in fetches[strips + 5 :]:
        copy.wait()

    @pl.when(slot == 1)
    def _():
        for copy in early:
            copy.wait_recv()
        order = [(h, f) for h in range(2) for f in range(fields)]
        value = y_spectra([jnp.concatenate([landed[j, h, f] for h, f in order], 0) for j in range(size)])
        for n, (h, f) in enumerate(order):
            acc[h, f] = value[n * each : (n + 1) * each]
        for h in range(2):
            propagate(acc.at[h], kept.at[h], h)
        value = y_fields(jnp.concatenate([kept[h, f] for h, f in order], 0))
        for j in range(size):
            for n, (h, f) in enumerate(order):
                leaving[j, h, f] = value[j][n * each : (n + 1) * each]
        for copy in back:
            copy.start()

    @pl.when(slot == 0)
    def _():
        ahead.wait_recv()

        def depart(h):
            for copies in late:
                copies[h].start()

        x_spectra(paired(fine, 0), wide_h, wide_l, put_mine, depart)
        for copies in late:
            for copy in copies:
                copy.wait_send()
        for copy in early:
            copy.wait_send()
        for copy in back:
            copy.wait_recv()

    @pl.when(slot == 1)
    def _():
        for h in range(2):
            for copies in late:
                copies[h].wait_recv()
            value = y_spectra(
                [jnp.concatenate([arrived[j, h, f] for f in range(fields)], 0) for j in range(size)]
            )
            for f in range(fields):
                acc[h, f] = value[f * each : (f + 1) * each] + kept[h, f]
            propagate(acc.at[h], change.at[h], h)
            value = y_fields(jnp.concatenate([change[h, f] for f in range(fields)], 0))
            for j in range(size):
                for f in range(fields):
                    going[j, h, f] = value[j][f * each : (f + 1) * each]
            for copies in home[1:]:
                copies[h].start()
            returned[me, h] = going[me, h]
        ahead.wait_send()
        for copy in back:
            copy.wait_send()

    for h in range(2):
        @pl.when(slot == 1)
        def _():
            for copies in home[1:]:
                copies[h].wait_recv()

        turned_up, turned_down = [], []
        for f in range(fields):
            spectrum = jnp.concatenate([returned[j, h, f] for j in range(size)], 0)
            for part, parts in zip(split(spectrum), (turned_up, turned_down)):
                flipped = dot(mirror[...], part, (1, 1)).astype(jnp.bfloat16)
                parts.append(jnp.concatenate([flipped[:rows], flipped[rows:]], 1))
        up, down = jnp.concatenate(turned_up, 0), jnp.concatenate(turned_down, 0)
        both = dot(jnp.concatenate([up, down], 0), ih[h])
        total = both[: up.shape[0]] + (both[up.shape[0] :] + dot(up, il[h]))
        sums[h] = total
    @pl.when(slot == 1)
    def _():
        for copies in home[1:]:
            for copy in copies:
                copy.wait_send()


def finish(fine, sums, out, held, sem):
    fields, strips, wide_rows, lanes = fine.shape
    rows = wide_rows // RATIO
    copies = []
    for n in range(strips):
        at = n % (strips // 2) * lanes
        even, odd = (sums[h, :, at : at + lanes] for h in range(2))
        change = even + odd if n < strips // 2 else even - odd
        for f in range(fields):
            for parity in range(RATIO):
                at = pl.ds(parity, rows, stride=RATIO)
                held[f, n, at] = fine[f, n, at] + change[f * rows : (f + 1) * rows]
        copies.append(
            pltpu.make_async_copy(held.at[:, n], out.at[:, :, pl.ds(n * lanes, lanes)], sem.at[n])
        )
        copies[-1].start()
    for copy in copies:
        copy.wait()


def shards(start_old, incoming):
    size = lax.axis_size("space")
    state = start_old[0]
    width = state.shape[2]
    fields, rows, nc = incoming.shape
    half = nc // 2
    count = half // size
    each = count // 2
    forward, wide, turn, twiddle, inverse, east, north, sine, versine = tables(nc)
    mirror = np.eye(2 * rows, dtype=np.float32)
    chipwise = lambda a: a.reshape(2, size, each, -1).transpose(1, 0, 2, 3).reshape(half, -1)
    east, sine, versine = chipwise(np.repeat(east[:, None], nc, axis=1)), chipwise(sine), chipwise(versine)
    north = np.repeat(north[None, :], 8, axis=0)
    operands = [state, incoming, mirror.astype(jnp.bfloat16), north, twiddle]
    distant = [*halves(wide), *halves(forward), *halves(turn), *halves(inverse)]
    strips = width // LANES
    padded = (fields, strips, state.shape[1] + 4 * HALO, LANES)
    blocks = (size, 2, fields, each, 2 * rows)
    whole = (2, fields, each, 2 * nc)
    shapes = [north.shape, twiddle.shape, (2, fields, HALO, width), padded, padded]
    shapes += [blocks] * 5 + [whole] * 3
    shapes += [blocks] * 3 + [(count, nc)] * 3
    buffers = [pltpu.VMEM(incoming.shape, jnp.float32)]
    buffers += [pltpu.VMEM(mirror.shape, jnp.bfloat16)]
    buffers += [pltpu.VMEM(shape, jnp.float32) for shape in shapes]
    far = pl.BlockSpec(memory_space=pltpu.HBM)
    inputs = len(operands) + len(distant) + 3
    dma = pltpu.SemaphoreType.DMA
    found = pl.pallas_call(
        functools.partial(kernel, size),
        out_shape=[
            pltpu.VMEM((fields, strips, state.shape[1], LANES), jnp.float32),
            pltpu.VMEM((2, fields * rows, width // 2), jnp.float32),
        ],
        in_specs=[far] * inputs,
        out_specs=[pl.BlockSpec(memory_space=pltpu.VMEM)] * 2,
        scratch_shapes=buffers
        + [pltpu.VMEM(table.shape, jnp.bfloat16) for table in distant]
        + [dma((inputs + strips,))]
        + [dma((2,))] * 2
        + [dma((1,))] * 2
        + [dma((size,))] * 4
        + [dma((size, 2))] * 4,
        compiler_params=pltpu.CompilerParams(
            collective_id=0, has_side_effects=True, vmem_limit_bytes=48 << 20
        ),
        cost_estimate=pl.CostEstimate(
            flops=40 * fields * count * nc * nc, bytes_accessed=32 * nc * nc, transcendentals=0
        ),
    )(*(pltpu.with_memory_space_constraint(a, pltpu.HBM) for a in (*operands, *distant, east, sine, versine)))
    result = pl.pallas_call(
        finish,
        out_shape=jax.ShapeDtypeStruct(state.shape, jnp.float32),
        in_specs=[pl.BlockSpec(memory_space=pltpu.VMEM)] * 2,
        out_specs=far,
        scratch_shapes=[pltpu.VMEM(found[0].shape, jnp.float32), dma((strips,))],
        compiler_params=pltpu.CompilerParams(vmem_limit_bytes=16 << 20),
    )(*(pltpu.with_memory_space_constraint(a, pltpu.VMEM) for a in found))
    return result[None]


def solution(mesh):
    placed = (P(("group", "tm"), None, "space", None), P("group", "space", None))
    return jax.shard_map(
        shards,
        mesh=mesh,
        in_specs=placed,
        out_specs=P(("group", "tm"), None, "space", None),
        check_vma=False,
    )
```
